32 devices in a mesh: row: 4 (over y, core), col: 8 (over z, x).
Axes of the slice: x: 2, y: 2, z: 4, core: 2. Of those that a mesh axis runs over, the one named last changes fastest.
Arguments:
- a_vals: bfloat16 [2, 8, 16, 5, 128, 128], P(None, 'row', 'col'), may hold values from -0.5 to 0.5
- a_off: int32 [2, 8, 16, 5], P(None, 'row', 'col'), may hold values from 0 to 8, as said below
- a_count: int32 [2, 8, 16], P(None, 'row', 'col'), may hold values from 1 to 5
- p_vals: bfloat16 [8, 16, 4, 128, 128], P('row', 'col'), may hold values from -1.1953125 to 1.1953125
Outputs:
- coarse: bfloat16 [2, 4, 8, 25, 128, 128], P(None, 'row', 'col')
The draws below stay inside these ranges and needn't reach their ends.
Inputs may be any that keep to these rules, and one draw needn't show every extreme that they name: Each row of a_off lists 5 different stencil positions of 0 to 8.
All inputs are finite; a program needn't handle non-finite values.
Results may differ from the reference program's by a relative error of at most 0.0049.
Values may be sent and summed in bfloat16 or wider, within the bound.
No kernel may reach another device: no remote copies, remote signals or barrier semaphores. Data moves between devices by JAX's collectives and lax.ppermute only.
A program may use at most 64 MiB of HBM per device.

```python
import jax
import jax.numpy as jnp
import numpy as np
from jax import lax

B = 128
KA = 5
OPS = 2
NXF = 8
NYF = 16


def draw_a_off(key, part):
    scores = jax.random.randint(key, (OPS, NXF, NYF, 9), 0, 1 << 20) * 16 + jnp.arange(9, dtype=jnp.int32)
    return jnp.argsort(scores, axis=-1)[..., :KA].astype(jnp.int32)


def set_ends(array, rng, smallest, largest):
    spot = [jax.random.randint(jax.random.fold_in(rng, axis), (), 0, length) for axis, length in enumerate(array.shape)]
    main_axis = array.shape.index(max(array.shape))
    next_to = spot[:main_axis] + [(spot[main_axis] + 1) % array.shape[main_axis]] + spot[main_axis + 1:]
    return array.at[tuple(spot)].set(smallest).at[tuple(next_to)].set(largest)


def block_levels(key, shape, split, least, top_value):
    loudness = 1.0
    for dim, parts in split:
        steps = jax.random.uniform(jax.random.fold_in(jax.random.fold_in(key, 6), dim), (parts,), jnp.float32, least / len(split), top_value / len(split))
        loudness = loudness * jnp.repeat(jnp.exp(steps), shape[dim] // parts).reshape((-1,) + (1,) * (len(shape) - 1 - dim))
    return loudness


def centred(stream_key, shape, width, reach, shards=(), kind=jnp.bfloat16):
    entries = width * jax.random.normal(stream_key, shape, jnp.float32)
    if shards:
        entries = entries * block_levels(stream_key, shape, shards, -0.22, 0.18)
    return jnp.clip(entries, -reach, reach).astype(kind)


def setup_inputs(seed: int = 0) -> dict:
    streams_of = jax.random.split(jax.random.key(seed), 5)
    return {
        "a_vals": centred(streams_of[0], (OPS, NXF, NYF, KA, B, B), B ** -0.5, 0.5, ((1, 4), (2, 8))),
        "a_off": draw_a_off(jax.random.fold_in(streams_of[4], 71), 0),
        "a_count": set_ends(jax.random.randint(streams_of[2], (OPS, NXF, NYF), 1, KA + 1), jax.random.fold_in(streams_of[2], 1), 1, KA).astype(jnp.int32),
        "p_vals": centred(streams_of[3], (NXF, NYF, 4, B, B), 0.2, 1.1953125, ((0, 4), (1, 8))),
    }


def coarse_table():
    band_table = np.zeros((16, 9, 25), np.float32)
    windows = []
    for lag_x in range(-1, 3):
        for lag_y in range(-1, 3):
            place = (lag_x + 1) * 4 + (lag_y + 1)
            corner_x = 1 if lag_x in (-1, 2) else 0
            corner_y = 1 if lag_y in (-1, 2) else 0
            windows.append((lag_x, lag_y, 2 * corner_x + corner_y))
            for step_x in range(3):
                for step_y in range(3):
                    target = (lag_x // 2 + step_x + 1) * 5 + (lag_y // 2 + step_y + 1)
                    band_table[place, step_x * 3 + step_y, target] = 1.0
    return band_table, windows


def band_index(near, anchor, corner):
    return jnp.floor_divide(near, 2) + corner * (2 * jnp.remainder(near, 2) - 1) - jnp.floor_divide(anchor, 2) + 1


def fine_products(blocks, slot_offsets, counts, p_vals):
    width_x, width_y = p_vals.shape[0], p_vals.shape[1]
    slot_total = blocks.shape[2]
    alive = (jnp.arange(slot_total, dtype=jnp.int32)[None, None, :] < counts[:, :, None]).astype(jnp.bfloat16)
    masked = blocks * alive[..., None, None]

    def one_row(row_index):
        row_blocks = masked[row_index].astype(jnp.float32)
        offsets = slot_offsets[row_index]
        near_x = row_index + offsets // 3 - 1
        anchor_y = jnp.arange(width_y, dtype=jnp.int32)[:, None]
        near_y = anchor_y + offsets % 3 - 1
        running = jnp.zeros(row_blocks.shape[:1] + (9,) + row_blocks.shape[2:], jnp.float32)
        for quadrant in range(4):
            picked = p_vals[jnp.remainder(near_x, width_x), jnp.remainder(near_y, width_y), quadrant].astype(jnp.float32)
            partial_terms = jnp.einsum('ykab,ykbc->ykac', row_blocks, picked)
            band = band_index(near_x, row_index, quadrant // 2) * 3 + band_index(near_y, anchor_y, quadrant % 2)
            onehot = (band[..., None] == jnp.arange(9, dtype=jnp.int32)).astype(jnp.float32)
            running = running + jnp.einsum('ykac,ykn->ynac', partial_terms, onehot)
        return running.astype(jnp.bfloat16)

    return lax.map(one_row, jnp.arange(width_x, dtype=jnp.int32))


def coarse_products(fine_w, p_vals):
    band_table, windows = coarse_table()
    width_x, width_y = p_vals.shape[0], p_vals.shape[1]
    coarse_cols = 2 * jnp.arange(width_y // 2, dtype=jnp.int32)

    def one_row(coarse_row):
        p_rows = jnp.stack([p_vals[jnp.remainder(2 * coarse_row + lag_x, width_x), jnp.remainder(coarse_cols + lag_y, width_y), quadrant] for lag_x, lag_y, quadrant in windows], axis=1)
        w_rows = jnp.stack([fine_w[:, jnp.remainder(2 * coarse_row + lag_x, width_x), jnp.remainder(coarse_cols + lag_y, width_y)] for lag_x, lag_y, quadrant in windows], axis=2)
        partial_terms = jnp.einsum('yuab,syujac->syujbc', p_rows.astype(jnp.float32), w_rows.astype(jnp.float32))
        summed = jnp.einsum('syujbc,ujn->synbc', partial_terms, jnp.asarray(band_table, dtype=jnp.float32))
        return summed.astype(jnp.bfloat16)

    rows_out = lax.map(one_row, jnp.arange(width_x // 2, dtype=jnp.int32))
    return jnp.moveaxis(rows_out, 0, 1)


def reference(a_vals, a_off, a_count, p_vals):
    fine_w = jnp.stack([fine_products(a_vals[operator], a_off[operator], a_count[operator], p_vals) for operator in range(a_vals.shape[0])])
    return coarse_products(fine_w, p_vals)
```

```python
import functools

import jax
import jax.numpy as jnp
from jax import lax
from jax.experimental import pallas as pl
from jax.experimental.pallas import tpu as pltpu
from jax.sharding import PartitionSpec as P

P_ROWS, P_COLS = 4, 6
A_COLS = 4
VMEM_LIMIT = 48 * 1024 * 1024


def ring(count, step):
    return [(i, (i + step) % count) for i in range(count)]


def pair(count):
    return [(i, i ^ 1) for i in range(count)]


def outward(count, width):
    return [(i, (i + (width if i % 2 else -width)) % count) for i in range(count)]


def onward(count):
    return [(i, (i + (-2 if i % 2 else 2)) % count) for i in range(count)]


def product_table(offsets, counts, zero_at):
    slots = offsets.shape[-1]
    shape = offsets.shape + (3, 3)
    dims = len(shape)
    fine_x = lax.broadcasted_iota(jnp.int32, shape, dims - 5)
    fine_y = lax.broadcasted_iota(jnp.int32, shape, dims - 4) - 1
    slot = lax.broadcasted_iota(jnp.int32, shape, dims - 3)
    band_y = lax.broadcasted_iota(jnp.int32, shape, dims - 2)
    band_x = lax.broadcasted_iota(jnp.int32, shape, dims - 1)
    off = offsets[..., None, None]
    near_x = fine_x + off // 3 - 1
    near_y = fine_y + off % 3 - 1
    first_x = ((near_x - 1) >> 1) - (fine_x >> 1) + 1
    first_y = ((near_y - 1) >> 1) - (fine_y >> 1) + 1
    place_x = band_x - first_x
    place_y = band_y - first_y
    corner_x = jnp.where(near_x & 1, place_x, 1 - place_x)
    corner_y = jnp.where(near_y & 1, place_y, 1 - place_y)
    good = (place_x >= 0) & (place_x < 2) & (place_y >= 0) & (place_y < 2)
    good = good & (slot < counts[..., None, None, None])
    index = ((near_x + 1) * P_COLS + near_y + 2) * 4 + 2 * corner_x + corner_y
    index = jnp.where(good, index, zero_at)
    return index.reshape(offsets.shape[:-3] + (2 * A_COLS * slots * 9,))


def load_window(odd, pieces, window, sems, number):
    copies = []
    for place, (rows, first) in enumerate(((2, 1), (1, 0), (1, 3))):
        own, near, far = pieces[3 * place : 3 * place + 3]
        for piece, col in ((own, 2), (near, jnp.where(odd, 0, 4)), (far, jnp.where(odd, 4, 0))):
            copies.append(
                pltpu.make_async_copy(
                    piece, window.at[pl.ds(first, rows), pl.ds(col, 2)], sems.at[number + len(copies)]
                )
            )
    return copies


def edge_kernel(operator, slots, table, odd_ref, a_own, a_near, a_far, *refs):
    pieces = refs[:9]
    low_ref, high_ref, w_ref, p_ref = refs[9:13]
    window, zero, blocks, sems = refs[13:]
    odd = odd_ref[0] == 1
    copies = load_window(odd, pieces, window, sems, 0)
    for src, col, width in ((a_own.at[operator], 1, 2), (a_near, jnp.where(odd, 0, 3), 1), (a_far, jnp.where(odd, 3, 0), 1)):
        copies.append(
            pltpu.make_async_copy(src, blocks.at[:, pl.ds(col, width)], sems.at[len(copies)])
        )
    for copy in copies:
        copy.start()
    block = zero.shape[-1]
    zero[...] = jnp.zeros(zero.shape, zero.dtype)
    for copy in copies:
        copy.wait()
    flat = p_ref
    for x in range(P_ROWS):
        for y in range(P_COLS):
            for q in range(4):
                flat[(x * P_COLS + y) * 4 + q] = window[x, y, q]
    flat[P_ROWS * P_COLS * 4] = zero[...]

    def one_row(row, carry):
        fine_x = row // A_COLS
        fine_y = row % A_COLS
        left = jnp.concatenate([blocks[fine_x, fine_y, k] for k in range(slots)], axis=1)
        for band_y in range(3):
            right = jnp.concatenate(
                [
                    jnp.concatenate(
                        [flat[table[((row * slots + k) * 3 + band_y) * 3 + band_x]] for band_x in range(3)],
                        axis=1,
                    )
                    for k in range(slots)
                ],
                axis=0,
            )
            w_ref[row, band_y] = jnp.dot(left, right, preferred_element_type=jnp.float32).astype(w_ref.dtype)
        return carry

    lax.fori_loop(0, 2 * A_COLS, one_row, 0)
    for out, fine_x in ((low_ref, 0), (high_ref, 1)):
        for lag_y in range(5):
            total = coarse_column(flat, w_ref, (fine_x,), lag_y, 2)
            for lag_x in range(3):
                out[lag_x, lag_y] = total[:, lag_x * block : (lag_x + 1) * block].astype(out.dtype)


def coarse_column(flat, w_ref, fine_rows, lag_y, corner_x):
    lefts, rights = [], []
    for fine_x in fine_rows:
        for col in range(A_COLS):
            fine_y = col - 1
            band_y = lag_y - (fine_y // 2 + 1)
            if 0 <= band_y < 3:
                corner_y = 1 if fine_y in (-1, 2) else 0
                lefts.append(flat[((fine_x + 1) * P_COLS + fine_y + 2) * 4 + corner_x + corner_y])
                rights.append(w_ref[fine_x * A_COLS + col, band_y])
    left = jnp.concatenate(lefts, axis=0)
    right = jnp.concatenate(rights, axis=0)
    return lax.dot_general(left, right, (((0,), (0,)), ((), ())), preferred_element_type=jnp.float32)


def own_kernel(flat, w_ref, out):
    block = out.shape[-1]
    for lag_y in range(5):
        total = coarse_column(flat, w_ref, (0, 1), lag_y, 0)
        for lag_x in range(3):
            out[lag_x, lag_y] = total[:, lag_x * block : (lag_x + 1) * block]


def final_kernel(*refs):
    out = refs[-1]
    for operator in range(out.shape[0]):
        own, low, high = refs[3 * operator : 3 * operator + 3]
        for lag_x in range(5):
            for lag_y in range(5):
                total = None
                for part, first in ((low, 0), (own, 1), (high, 2)):
                    if 0 <= lag_x - first < 3:
                        term = part[lag_x - first, lag_y].astype(jnp.float32)
                        total = term if total is None else total + term
                out[operator, 0, 0, 5 * lag_x + lag_y] = total.astype(out.dtype)


def per_device(a_vals, a_off, a_count, p_vals):
    operators, _, _, slots, block, _ = a_vals.shape
    cols = lax.axis_size("col")
    rows = lax.axis_size("row")
    odd = lax.axis_index("col") % 2
    up, down = ring(rows, 1), ring(rows, -1)
    near_way, far_way, on_way = pair(cols), outward(cols, 1), onward(cols)

    def both_rows(piece):
        low = lax.ppermute(piece[1:2], "row", up)
        high = lax.ppermute(piece[0:1], "row", down)
        return low, high

    def facing(array, dim, index):
        return lax.dynamic_slice_in_dim(array, index, 1, axis=dim)

    info = jnp.concatenate([a_off, a_count[..., None]], axis=-1)
    p_near = lax.ppermute(p_vals, "col", near_way)
    info_near = lax.ppermute(facing(info, 2, 1 - odd), "col", near_way)
    info_far = lax.ppermute(facing(info, 2, odd), "col", far_way)
    own_low, own_high = both_rows(p_vals)
    a_near, a_far = [], []
    for operator in range(operators):
        a_near.append(lax.ppermute(facing(a_vals[operator], 1, 1 - odd), "col", near_way))
        a_far.append(lax.ppermute(facing(a_vals[operator], 1, odd), "col", far_way))
    p_far = lax.ppermute(p_near, "col", on_way)
    near_low, near_high = both_rows(p_near)
    far_low, far_high = both_rows(p_far)
    pieces = (p_vals, p_near, p_far, own_low, near_low, far_low, own_high, near_high, far_high)

    left = jnp.where(odd == 1, info_near, info_far)
    right = jnp.where(odd == 1, info_far, info_near)
    info_all = jnp.concatenate([left, info, right], axis=2)
    zero_at = P_ROWS * P_COLS * 4
    table = product_table(info_all[..., :slots], info_all[..., slots], zero_at)
    odd_arg = odd.astype(jnp.int32)[None]

    any_spec = pl.BlockSpec(memory_space=pl.ANY)
    smem = pl.BlockSpec(memory_space=pltpu.SMEM)
    vmem = pl.BlockSpec(memory_space=pltpu.VMEM)
    bf16, f32 = jnp.bfloat16, jnp.float32
    params = pltpu.CompilerParams(vmem_limit_bytes=VMEM_LIMIT)
    partial_shape = jax.ShapeDtypeStruct((3, 5, block, block), bf16)
    finals = []
    for operator in range(operators):
        low, high, w_all, flat = pl.pallas_call(
            functools.partial(edge_kernel, operator, slots),
            in_specs=[smem, smem] + [any_spec] * 12,
            out_specs=[vmem] * 4,
            out_shape=[
                partial_shape,
                partial_shape,
                jax.ShapeDtypeStruct((2 * A_COLS, 3, block, 3 * block), bf16),
                jax.ShapeDtypeStruct((zero_at + 1, block, block), bf16),
            ],
            scratch_shapes=[
                pltpu.VMEM((P_ROWS, P_COLS, 4, block, block), bf16),
                pltpu.VMEM((block, block), bf16),
                pltpu.VMEM((2, A_COLS, slots, block, block), bf16),
                pltpu.SemaphoreType.DMA((12,)),
            ],
            compiler_params=params,
            cost_estimate=pl.CostEstimate(flops=500 * 2 * block**3, bytes_accessed=8 << 20, transcendentals=0),
            name="edge",
        )(table[operator], odd_arg, a_vals, a_near[operator], a_far[operator], *pieces)
        from_low = lax.ppermute(high, "row", up)
        from_high = lax.ppermute(low, "row", down)
        own = pl.pallas_call(
            own_kernel,
            in_specs=[vmem] * 2,
            out_specs=vmem,
            out_shape=jax.ShapeDtypeStruct((3, 5, block, block), f32),
            compiler_params=params,
            cost_estimate=pl.CostEstimate(flops=100 * 2 * block**3, bytes_accessed=6 << 20, transcendentals=0),
            name="own",
        )(flat, w_all)
        finals += [own, from_low, from_high]
    return pl.pallas_call(
        final_kernel,
        in_specs=[vmem] * len(finals),
        out_specs=vmem,
        out_shape=jax.ShapeDtypeStruct((operators, 1, 1, 25, block, block), bf16),
        compiler_params=params,
        cost_estimate=pl.CostEstimate(flops=1 << 20, bytes_accessed=8 << 20, transcendentals=0),
        name="final",
    )(*finals)


def solution(mesh):
    placed = (
        P(None, "row", "col", None, None, None),
        P(None, "row", "col", None),
        P(None, "row", "col"),
        P("row", "col", None, None, None),
    )
    return jax.shard_map(
        per_device,
        mesh=mesh,
        in_specs=placed,
        out_specs=P(None, "row", "col", None, None, None),
        check_vma=False,
    )
```

```python
import functools

import jax
import jax.numpy as jnp
from jax import lax
from jax.experimental import pallas as pl
from jax.experimental.pallas import tpu as pltpu
from jax.sharding import PartitionSpec as P

FAR, OWN_0, OWN_1, NEAR = range(4)
HALF = 32
ZERO = 2 * HALF
VMEM_LIMIT = 24 * 1024 * 1024


def ring(count, step):
    return [(i, (i + step) % count) for i in range(count)]


def pair(count):
    return [(i, i ^ 1) for i in range(count)]


def outward(count):
    return [(i, (i + (1 if i % 2 else -1)) % count) for i in range(count)]


def onward(count):
    return [(i, (i + (-2 if i % 2 else 2)) % count) for i in range(count)]


def product_table(info, odd):
    slots = info.shape[1] - 1
    shape = (info.shape[0], slots * 9)
    row = lax.broadcasted_iota(jnp.int32, shape, 0)
    place = lax.broadcasted_iota(jnp.int32, shape, 1)
    slot = place // 9
    band = place - 9 * slot
    band_y = band // 3
    band_x = band - 3 * band_y
    fine_x = (row >> 2) & 1
    fine_y = (row & 3) - 1
    off = jnp.zeros(shape, jnp.int32)
    for k in range(slots):
        off = off + jnp.where(slot == k, info[:, k : k + 1], 0)
    off_x = off // 3
    near_x = fine_x + off_x - 1
    near_y = fine_y + (off - 3 * off_x - 1) * (1 - 2 * odd)
    place_x = band_x - (((near_x - 1) >> 1) - (fine_x >> 1) + 1)
    place_y = band_y - (((near_y - 1) >> 1) - (fine_y >> 1) + 1)
    corner_x = jnp.where((near_x & 1) == 1, place_x, 1 - place_x)
    corner_y = jnp.where((near_y & 1) == 1, place_y, 1 - place_y)
    good = (place_x >= 0) & (place_x < 2) & (place_y >= 0) & (place_y < 2)
    good = good & (slot < info[:, slots:])
    side = jnp.where((near_y >> 1) == 0, 0, HALF)
    index = side + (near_x + 1) * 8 + ((near_y & 1) ^ odd) * 4 + 2 * corner_x + corner_y
    return jnp.where(good, index, ZERO)


def fill(flat, sems, first, low, mid, high):
    block = flat.shape[-1]
    copies = []
    for piece, start, rows in ((low, 0, 1), (mid, 8, 2), (high, 24, 1)):
        for x in range(rows):
            for y in range(2):
                copies.append((piece.at[x, y], flat.at[pl.ds(first + start + 8 * x + 4 * y, 4)]))
    return [pltpu.make_async_copy(src, dst, sems.at[first // 4 + i]) for i, (src, dst) in enumerate(copies)]


def fine_row(table, number, flat, blocks, w_ref):
    slots = blocks.shape[0]
    left = jnp.concatenate([blocks[k] for k in range(slots)], axis=1)
    for band_y in range(3):
        right = jnp.concatenate(
            [
                jnp.concatenate(
                    [flat[table[number, k * 9 + band_y * 3 + band_x]] for band_x in range(3)], axis=1
                )
                for k in range(slots)
            ],
            axis=0,
        )
        w_ref[band_y] = jnp.dot(left, right, preferred_element_type=jnp.float32).astype(w_ref.dtype)


def coarse_column(odd, pieces, w_refs, fine_rows, lag_y, corner_x):
    lefts, rights = [], []
    for fine_x in fine_rows:
        for role in range(4):
            fine_y = role - 1
            band_y = lag_y - (fine_y // 2 + 1)
            if 0 <= band_y < 3:
                corner_y = 1 if role in (FAR, NEAR) else 0
                lefts.append(pieces[role][fine_x, (fine_y & 1) ^ odd, corner_x + corner_y])
                rights.append(w_refs[role][fine_x, band_y])
    left = jnp.concatenate(lefts, axis=0)
    right = jnp.concatenate(rights, axis=0)
    return lax.dot_general(left, right, (((0,), (0,)), ((), ())), preferred_element_type=jnp.float32)


def edges(odd, pieces, w_refs, outs):
    block = outs[0].shape[-1]
    for fine_x, out in enumerate(outs):
        for lag_y in range(5):
            total = coarse_column(odd, pieces, w_refs, (fine_x,), lag_y, 2)
            for lag_x in range(3):
                out[lag_x, lag_y] = total[:, lag_x * block : (lag_x + 1) * block].astype(out.dtype)


def near_own_kernel(table, odd_ref, a_own, *refs):
    own, near = refs[:3], refs[3:6]
    flat, w_ref = refs[6:8]
    blocks, sems = refs[8:]
    odd = odd_ref[0]
    operators = a_own.shape[0]
    copies = fill(flat, sems, 0, *own) + fill(flat, sems, HALF, *near)
    copies.append(pltpu.make_async_copy(a_own.at[:, :, 1 - odd], blocks, sems.at[16]))
    for copy in copies:
        copy.start()
    flat[ZERO] = jnp.zeros(flat.shape[1:], flat.dtype)
    for copy in copies:
        copy.wait()

    def one(i, carry):
        s, x = i >> 1, i & 1
        fine_row(table, s * 8 + x * 4 + OWN_1, flat, blocks.at[s, x], w_ref.at[s, x])
        return carry

    lax.fori_loop(0, 2 * operators, one, 0)


def near_kernel(operator, table, flat, a_near, w_ref):
    def one(x, carry):
        fine_row(table, operator * 8 + x * 4 + NEAR, flat, a_near.at[x, 0], w_ref.at[x])
        return carry

    lax.fori_loop(0, 2, one, 0)


def far_first_kernel(table, odd_ref, a_own, a_far, w_own, w_near, p_own, p_near, p_far, *refs):
    own, far = refs[:3], refs[3:6]
    low, high, flat, w_own_0, w_far = refs[6:11]
    blocks, sems = refs[11:]
    odd = odd_ref[0]
    copies = fill(flat, sems, 0, *own) + fill(flat, sems, HALF, *far)
    copies.append(pltpu.make_async_copy(a_own.at[0, :, odd], blocks, sems.at[16]))
    for copy in copies:
        copy.start()
    flat[ZERO] = jnp.zeros(flat.shape[1:], flat.dtype)
    for copy in copies:
        copy.wait()

    def one(x, carry):
        fine_row(table, x * 4 + FAR, flat, a_far.at[x, 0], w_far.at[x])
        fine_row(table, x * 4 + OWN_0, flat, blocks.at[x], w_own_0.at[x])
        return carry

    lax.fori_loop(0, 2, one, 0)
    edges(odd, (p_far, p_own, p_own, p_near), (w_far, w_own_0, w_own.at[0], w_near), (low, high))


def own_0_kernel(operator, table, odd_ref, a_own, flat, w_ref, blocks, sem):
    odd = odd_ref[0]
    copy = pltpu.make_async_copy(a_own.at[operator, :, odd], blocks, sem)
    copy.start()
    copy.wait()

    def one(x, carry):
        fine_row(table, operator * 8 + x * 4 + OWN_0, flat, blocks.at[x], w_ref.at[x])
        return carry

    lax.fori_loop(0, 2, one, 0)


def far_kernel(operator, table, odd_ref, a_far, flat, w_own, w_near, w_own_0, p_own, p_near, p_far, low, high, w_far):
    odd = odd_ref[0]

    def one(x, carry):
        fine_row(table, operator * 8 + x * 4 + FAR, flat, a_far.at[x, 0], w_far.at[x])
        return carry

    lax.fori_loop(0, 2, one, 0)
    edges(odd, (p_far, p_own, p_own, p_near), (w_far, w_own_0, w_own.at[operator], w_near), (low, high))


def centre_kernel(operator, odd_ref, p_own, p_near, p_far, w_far, w_own_0, w_own, w_near, out):
    block = out.shape[-1]
    odd = odd_ref[0]
    for lag_y in range(5):
        total = coarse_column(
            odd, (p_far, p_own, p_own, p_near), (w_far, w_own_0, w_own.at[operator], w_near), (0, 1), lag_y, 0
        )
        for lag_x in range(3):
            out[lag_x, lag_y] = total[:, lag_x * block : (lag_x + 1) * block]


def final_kernel(odd_ref, *refs):
    out = refs[-1]
    odd = odd_ref[0]
    for operator in range(out.shape[0]):
        own, low, high = refs[3 * operator : 3 * operator + 3]
        for lag_x in range(5):
            for lag_y in range(5):
                total = None
                for part, first in ((low, 0), (own, 1), (high, 2)):
                    if 0 <= lag_x - first < 3:
                        term = part[lag_x - first, lag_y].astype(jnp.float32)
                        total = term if total is None else total + term
                place = 5 * lag_x + lag_y + odd * (4 - 2 * lag_y)
                out[operator, 0, 0, place] = total.astype(out.dtype)


def per_device(a_vals, a_off, a_count, p_vals):
    operators, _, _, slots, block, _ = a_vals.shape
    cols = lax.axis_size("col")
    rows = lax.axis_size("row")
    odd = (lax.axis_index("col") & 1).astype(jnp.int32)
    up, down = ring(rows, 1), ring(rows, -1)
    near_way, far_way, on_way = pair(cols), outward(cols), onward(cols)

    def both_rows(piece):
        return lax.ppermute(piece[1:2], "row", up), lax.ppermute(piece[0:1], "row", down)

    def column(array, operator, index):
        zero = jnp.int32(0)
        start = (jnp.int32(operator), zero, index) + (zero,) * (array.ndim - 3)
        return lax.dynamic_slice(array, start, (1, 2, 1) + array.shape[3:])[0]

    p_near = lax.ppermute(p_vals, "col", near_way)
    own_low, own_high = both_rows(p_vals)

    info = jnp.concatenate([a_off, a_count[..., None]], axis=-1)
    info_near = lax.ppermute(lax.dynamic_slice_in_dim(info, 1 - odd, 1, axis=2), "col", near_way)
    info_far = lax.ppermute(lax.dynamic_slice_in_dim(info, odd, 1, axis=2), "col", far_way)
    mirrored = jnp.where(odd == 1, info[:, :, ::-1], info)
    table = product_table(
        jnp.concatenate([info_far, mirrored, info_near], axis=2).reshape(operators * 8, slots + 1), odd
    )

    near_sends = [column(a_vals, s, 1 - odd) for s in range(operators)]
    far_sends = [column(a_vals, s, odd) for s in range(operators)]
    p_near, near_sends, far_sends = lax.optimization_barrier((p_near, near_sends, far_sends))
    p_far = lax.ppermute(p_near, "col", on_way)
    near_low, near_high = both_rows(p_near)
    a_near, a_far = [None] * operators, [None] * operators
    a_near[0] = lax.ppermute(near_sends[0], "col", near_way)
    a_far[0] = lax.ppermute(far_sends[0], "col", far_way)
    p_far, later_near, later_far = lax.optimization_barrier((p_far, near_sends[1:], far_sends[1:]))
    far_low, far_high = both_rows(p_far)
    for s in range(1, operators):
        a_near[s] = lax.ppermute(later_near[s - 1], "col", near_way)
        a_far[s] = lax.ppermute(later_far[s - 1], "col", far_way)

    any_spec = pl.BlockSpec(memory_space=pl.ANY)
    smem = pl.BlockSpec(memory_space=pltpu.SMEM)
    vmem = pl.BlockSpec(memory_space=pltpu.VMEM)
    bf16, f32 = jnp.bfloat16, jnp.float32
    odd_arg = odd[None]
    flat_shape = jax.ShapeDtypeStruct((ZERO + 1, block, block), bf16)
    w_shape = jax.ShapeDtypeStruct((2, 3, block, 3 * block), bf16)
    part_shape = jax.ShapeDtypeStruct((3, 5, block, block), bf16)
    own_pieces = (own_low, p_vals, own_high)

    def call(kernel, in_specs, out_shape, products, scratch=(), name=None):
        single = not isinstance(out_shape, list)
        return pl.pallas_call(
            kernel,
            in_specs=in_specs,
            out_specs=vmem if single else [vmem] * len(out_shape),
            out_shape=out_shape,
            scratch_shapes=list(scratch),
            compiler_params=pltpu.CompilerParams(vmem_limit_bytes=VMEM_LIMIT),
            cost_estimate=pl.CostEstimate(flops=products * 2 * block**3, bytes_accessed=4 << 20, transcendentals=0),
            name=name,
        )

    flat_near, w_own = call(
        near_own_kernel,
        [smem, smem] + [any_spec] * 7,
        [flat_shape, jax.ShapeDtypeStruct((operators,) + w_shape.shape, bf16)],
        360,
        [pltpu.VMEM((operators, 2, slots, block, block), bf16), pltpu.SemaphoreType.DMA((17,))],
        "near_own",
    )(table, odd_arg, a_vals, *own_pieces, near_low, p_near, near_high)

    finals = []
    for s in range(operators):
        w_near = call(functools.partial(near_kernel, s), [smem, vmem, vmem], w_shape, 90, (), "near")(
            table, flat_near, a_near[s]
        )
        if s == 0:
            low, high, flat_far, w_own_0, w_far = call(
                far_first_kernel,
                [smem, smem, any_spec, vmem, vmem, vmem, vmem, vmem, vmem] + [any_spec] * 6,
                [part_shape, part_shape, flat_shape, w_shape, w_shape],
                300,
                [pltpu.VMEM((2, slots, block, block), bf16), pltpu.SemaphoreType.DMA((17,))],
                "far_first",
            )(
                table, odd_arg, a_vals, a_far[s], w_own, w_near, p_vals, p_near, p_far,
                *own_pieces, far_low, p_far, far_high,
            )
        else:
            w_own_0 = call(
                functools.partial(own_0_kernel, s),
                [smem, smem, any_spec, vmem],
                w_shape,
                90,
                [pltpu.VMEM((2, slots, block, block), bf16), pltpu.SemaphoreType.DMA],
                "own_0",
            )(table, odd_arg, a_vals, flat_far)
            low, high, w_far = call(
                functools.partial(far_kernel, s),
                [smem, smem] + [vmem] * 8,
                [part_shape, part_shape, w_shape],
                200,
                (),
                "far",
            )(table, odd_arg, a_far[s], flat_far, w_own, w_near, w_own_0, p_vals, p_near, p_far)
        from_low = lax.ppermute(high, "row", up)
        from_high = lax.ppermute(low, "row", down)
        centre = call(
            functools.partial(centre_kernel, s),
            [smem] + [vmem] * 7,
            jax.ShapeDtypeStruct((3, 5, block, block), f32),
            144,
            (),
            "centre",
        )(odd_arg, p_vals, p_near, p_far, w_far, w_own_0, w_own, w_near)
        finals += [centre, from_low, from_high]
    return call(
        final_kernel,
        [smem] + [vmem] * len(finals),
        jax.ShapeDtypeStruct((operators, 1, 1, 25, block, block), bf16),
        1,
        (),
        "final",
    )(odd_arg, *finals)


def solution(mesh):
    placed = (
        P(None, "row", "col", None, None, None),
        P(None, "row", "col", None),
        P(None, "row", "col"),
        P("row", "col", None, None, None),
    )
    return jax.shard_map(
        per_device,
        mesh=mesh,
        in_specs=placed,
        out_specs=P(None, "row", "col", None, None, None),
        check_vma=False,
    )
```

```python
import functools

import jax
import jax.numpy as jnp
from jax import lax
from jax.experimental import pallas as pl
from jax.experimental.pallas import tpu as pltpu
from jax.sharding import PartitionSpec as P

FAR, OWN_0, OWN_1, NEAR = range(4)
HALF = 32
ZERO = 3 * HALF
VMEM_LIMIT = 24 * 1024 * 1024


def ring(count, step):
    return [(i, (i + step) % count) for i in range(count)]


def pair(count):
    return [(i, i ^ 1) for i in range(count)]


def outward(count):
    return [(i, (i + (1 if i % 2 else -1)) % count) for i in range(count)]


def onward(count):
    return [(i, (i + (-2 if i % 2 else 2)) % count) for i in range(count)]


def product_table(info, odd):
    slots = info.shape[1] - 1
    shape = (info.shape[0], slots * 9)
    row = lax.broadcasted_iota(jnp.int32, shape, 0)
    place = lax.broadcasted_iota(jnp.int32, shape, 1)
    slot = place // 9
    band = place - 9 * slot
    band_y = band // 3
    band_x = band - 3 * band_y
    fine_x = (row >> 2) & 1
    fine_y = (row & 3) - 1
    off = jnp.zeros(shape, jnp.int32)
    for k in range(slots):
        off = off + jnp.where(slot == k, info[:, k : k + 1], 0)
    off_x = off // 3
    near_x = fine_x + off_x - 1
    near_y = fine_y + (off - 3 * off_x - 1) * (1 - 2 * odd)
    place_x = band_x - (((near_x - 1) >> 1) - (fine_x >> 1) + 1)
    place_y = band_y - (((near_y - 1) >> 1) - (fine_y >> 1) + 1)
    corner_x = jnp.where((near_x & 1) == 1, place_x, 1 - place_x)
    corner_y = jnp.where((near_y & 1) == 1, place_y, 1 - place_y)
    good = (place_x >= 0) & (place_x < 2) & (place_y >= 0) & (place_y < 2)
    good = good & (slot < info[:, slots:])
    side = jnp.where(near_y < 0, 2 * HALF, jnp.where(near_y < 2, 0, HALF))
    index = side + (near_x + 1) * 8 + ((near_y & 1) ^ odd) * 4 + 2 * corner_x + corner_y
    return jnp.where(good, index, ZERO)


def fill(flat, first, low, mid, high):
    for piece, start in ((low, 0), (mid, 8), (high, 24)):
        for x in range(piece.shape[0]):
            for y in range(2):
                flat[pl.ds(first + start + 8 * x + 4 * y, 4)] = piece[x, y]


def pack_kernel(odd_ref, a_own, info, *refs):
    sems = refs[-1]
    operators = a_own.shape[0]
    odd = odd_ref[0]
    info_near, info_far = refs[2 * operators : 2 * operators + 2]
    copies = []
    for s in range(operators):
        copies.append((a_own.at[s, :, pl.ds(1 - odd, 1)], refs[s]))
        copies.append((a_own.at[s, :, pl.ds(odd, 1)], refs[operators + s]))
    copies = [pltpu.make_async_copy(src, dst, sems.at[i]) for i, (src, dst) in enumerate(copies)]
    for copy in copies:
        copy.start()
    info_near[...] = info[:, :, pl.ds(1 - odd, 1)]
    info_far[...] = info[:, :, pl.ds(odd, 1)]
    for copy in copies:
        copy.wait()


def rows_kernel(own, near, low, high):
    for out, x in ((low, 0), (high, 1)):
        out[0, 0:2] = own[x]
        out[0, 2:4] = near[x]


def fine_row(table, number, flat, blocks, w_ref):
    slots = blocks.shape[0]
    left = jnp.concatenate([blocks[k] for k in range(slots)], axis=1)
    for band_y in range(3):
        right = jnp.concatenate(
            [
                jnp.concatenate(
                    [flat[table[number, k * 9 + band_y * 3 + band_x]] for band_x in range(3)], axis=1
                )
                for k in range(slots)
            ],
            axis=0,
        )
        w_ref[band_y] = jnp.dot(left, right, preferred_element_type=jnp.float32).astype(w_ref.dtype)


def coarse_column(odd, pieces, w_refs, fine_rows, lag_y, corner_x):
    lefts, rights = [], []
    for fine_x in fine_rows:
        for role in range(4):
            fine_y = role - 1
            band_y = lag_y - (fine_y // 2 + 1)
            if 0 <= band_y < 3:
                corner_y = 1 if role in (FAR, NEAR) else 0
                lefts.append(pieces[role][fine_x, (fine_y & 1) ^ odd, corner_x + corner_y])
                rights.append(w_refs[role][fine_x, band_y])
    left = jnp.concatenate(lefts, axis=0)
    right = jnp.concatenate(rights, axis=0)
    return lax.dot_general(left, right, (((0,), (0,)), ((), ())), preferred_element_type=jnp.float32)


def edges(odd, pieces, w_refs, outs):
    block = outs[0].shape[-1]
    for fine_x, out in enumerate(outs):
        for lag_y in range(5):
            total = coarse_column(odd, pieces, w_refs, (fine_x,), lag_y, 2)
            for lag_x in range(3):
                out[lag_x, lag_y] = total[:, lag_x * block : (lag_x + 1) * block].astype(out.dtype)


def near_own_kernel(table, odd_ref, a_own, p_own, p_near, low, high, flat, w_ref):
    odd = odd_ref[0]
    fill(flat, 0, low.at[:, 0:2], p_own, high.at[:, 0:2])
    fill(flat, HALF, low.at[:, 2:4], p_near, high.at[:, 2:4])
    flat[ZERO] = jnp.zeros(flat.shape[1:], flat.dtype)
    for s in range(a_own.shape[0]):
        for x in range(2):
            fine_row(table, s * 8 + x * 4 + OWN_1, flat, a_own.at[s, x, 1 - odd], w_ref.at[s, x])


def near_kernel(operator, table, flat, a_near, w_ref):
    for x in range(2):
        fine_row(table, operator * 8 + x * 4 + NEAR, flat, a_near.at[x, 0], w_ref.at[x])


def far_first_kernel(
    table, odd_ref, a_own, a_far, w_own, w_near, p_own, p_near, p_far, far_low, far_high, held, low, high, flat, w_own_0, w_far
):
    odd = odd_ref[0]
    fill(flat, 2 * HALF, far_low, p_far, far_high)
    for x in range(2):
        fine_row(table, x * 4 + FAR, flat, a_far.at[x, 0], w_far.at[x])
        fine_row(table, x * 4 + OWN_0, flat, a_own.at[0, x, odd], w_own_0.at[x])
    edges(odd, (p_far, p_own, p_own, p_near), (w_far, w_own_0, w_own.at[0], w_near), (low, high))


def own_0_kernel(operator, table, odd_ref, a_own, flat, w_ref):
    odd = odd_ref[0]
    for x in range(2):
        fine_row(table, operator * 8 + x * 4 + OWN_0, flat, a_own.at[operator, x, odd], w_ref.at[x])


def far_kernel(operator, table, odd_ref, a_far, flat, w_own, w_near, w_own_0, p_own, p_near, p_far, low, high, w_far):
    odd = odd_ref[0]
    for x in range(2):
        fine_row(table, operator * 8 + x * 4 + FAR, flat, a_far.at[x, 0], w_far.at[x])
    edges(odd, (p_far, p_own, p_own, p_near), (w_far, w_own_0, w_own.at[operator], w_near), (low, high))


def centre_kernel(operator, odd_ref, p_own, p_near, p_far, w_far, w_own_0, w_own, w_near, out):
    block = out.shape[-1]
    odd = odd_ref[0]
    for lag_y in range(5):
        total = coarse_column(
            odd, (p_far, p_own, p_own, p_near), (w_far, w_own_0, w_own.at[operator], w_near), (0, 1), lag_y, 0
        )
        for lag_x in range(3):
            out[lag_x, lag_y] = total[:, lag_x * block : (lag_x + 1) * block]


def final_kernel(odd_ref, *refs):
    out = refs[-1]
    odd = odd_ref[0]
    for operator in range(out.shape[0]):
        own, low, high = refs[3 * operator : 3 * operator + 3]
        for lag_x in range(5):
            for lag_y in range(5):
                total = None
                for part, first in ((low, 0), (own, 1), (high, 2)):
                    if 0 <= lag_x - first < 3:
                        term = part[lag_x - first, lag_y].astype(jnp.float32)
                        total = term if total is None else total + term
                place = 5 * lag_x + lag_y + odd * (4 - 2 * lag_y)
                out[operator, 0, 0, place] = total.astype(out.dtype)


def per_device(a_vals, a_off, a_count, p_vals):
    operators, _, _, slots, block, _ = a_vals.shape
    cols = lax.axis_size("col")
    rows = lax.axis_size("row")
    odd = (lax.axis_index("col") & 1).astype(jnp.int32)
    up, down = ring(rows, 1), ring(rows, -1)
    near_way, far_way, on_way = pair(cols), outward(cols), onward(cols)

    any_spec = pl.BlockSpec(memory_space=pl.ANY)
    smem = pl.BlockSpec(memory_space=pltpu.SMEM)
    vmem = pl.BlockSpec(memory_space=pltpu.VMEM)
    bf16, f32 = jnp.bfloat16, jnp.float32
    odd_arg = odd[None]
    flat_shape = jax.ShapeDtypeStruct((ZERO + 1, block, block), bf16)
    w_shape = jax.ShapeDtypeStruct((2, 3, block, 3 * block), bf16)
    part_shape = jax.ShapeDtypeStruct((3, 5, block, block), bf16)

    def call(kernel, in_specs, out_shape, products, name, scratch=(), aliases=None):
        single = not isinstance(out_shape, list)
        return pl.pallas_call(
            kernel,
            in_specs=in_specs,
            out_specs=vmem if single else [vmem] * len(out_shape),
            out_shape=out_shape,
            scratch_shapes=list(scratch),
            input_output_aliases=aliases or {},
            compiler_params=pltpu.CompilerParams(vmem_limit_bytes=VMEM_LIMIT),
            cost_estimate=pl.CostEstimate(flops=products * 2 * block**3, bytes_accessed=4 << 20, transcendentals=0),
            name=name,
        )

    p_near = lax.ppermute(p_vals, "col", near_way)
    info = jnp.concatenate([a_off, a_count[..., None]], axis=-1)
    column = jax.ShapeDtypeStruct((2, 1, slots, block, block), bf16)
    info_column = jax.ShapeDtypeStruct((operators, 2, 1, slots + 1), jnp.int32)
    *sends, info_near, info_far = call(
        pack_kernel,
        [smem, any_spec, vmem],
        [column] * (2 * operators) + [info_column] * 2,
        1,
        "pack",
        [pltpu.SemaphoreType.DMA((2 * operators,))],
    )(odd_arg, a_vals, info)
    info_near = lax.ppermute(info_near, "col", near_way)
    info_far = lax.ppermute(info_far, "col", far_way)
    mirrored = jnp.where(odd == 1, info[:, :, ::-1], info)
    table = product_table(
        jnp.concatenate([info_far, mirrored, info_near], axis=2).reshape(operators * 8, slots + 1), odd
    )

    p_near, sends = lax.optimization_barrier((p_near, sends))
    near_sends, far_sends = sends[:operators], sends[operators:]
    p_far = lax.ppermute(p_near, "col", on_way)
    row_shape = jax.ShapeDtypeStruct((1, 4, 4, block, block), bf16)
    low, high = call(rows_kernel, [vmem, vmem], [row_shape, row_shape], 1, "rows")(p_vals, p_near)
    from_low = lax.ppermute(high, "row", up)
    from_high = lax.ppermute(low, "row", down)
    a_near, a_far = [None] * operators, [None] * operators
    a_near[0] = lax.ppermute(near_sends[0], "col", near_way)
    a_far[0] = lax.ppermute(far_sends[0], "col", far_way)
    p_far, later_near, later_far = lax.optimization_barrier((p_far, near_sends[1:], far_sends[1:]))
    far_low = lax.ppermute(p_far[1:2], "row", up)
    far_high = lax.ppermute(p_far[0:1], "row", down)
    for s in range(1, operators):
        a_near[s] = lax.ppermute(later_near[s - 1], "col", near_way)
        a_far[s] = lax.ppermute(later_far[s - 1], "col", far_way)

    flat, w_own = call(
        near_own_kernel,
        [smem, smem] + [vmem] * 5,
        [flat_shape, jax.ShapeDtypeStruct((operators,) + w_shape.shape, bf16)],
        360,
        "near_own",
    )(table, odd_arg, a_vals, p_vals, p_near, from_low, from_high)

    finals = []
    for s in range(operators):
        w_near = call(functools.partial(near_kernel, s), [smem, vmem, vmem], w_shape, 90, "near")(
            table, flat, a_near[s]
        )
        if s == 0:
            low, high, flat, w_own_0, w_far = call(
                far_first_kernel,
                [smem, smem] + [vmem] * 10,
                [part_shape, part_shape, flat_shape, w_shape, w_shape],
                300,
                "far_first",
                aliases={11: 2},
            )(table, odd_arg, a_vals, a_far[s], w_own, w_near, p_vals, p_near, p_far, far_low, far_high, flat)
        else:
            w_own_0 = call(functools.partial(own_0_kernel, s), [smem, smem, vmem, vmem], w_shape, 90, "own_0")(
                table, odd_arg, a_vals, flat
            )
            low, high, w_far = call(
                functools.partial(far_kernel, s),
                [smem, smem] + [vmem] * 8,
                [part_shape, part_shape, w_shape],
                200,
                "far",
            )(table, odd_arg, a_far[s], flat, w_own, w_near, w_own_0, p_vals, p_near, p_far)
        from_low = lax.ppermute(high, "row", up)
        from_high = lax.ppermute(low, "row", down)
        centre = call(
            functools.partial(centre_kernel, s),
            [smem] + [vmem] * 7,
            jax.ShapeDtypeStruct((3, 5, block, block), f32),
            144,
            "centre",
        )(odd_arg, p_vals, p_near, p_far, w_far, w_own_0, w_own, w_near)
        finals += [centre, from_low, from_high]
    return call(
        final_kernel,
        [smem] + [vmem] * len(finals),
        jax.ShapeDtypeStruct((operators, 1, 1, 25, block, block), bf16),
        1,
        "final",
    )(odd_arg, *finals)


def solution(mesh):
    placed = (
        P(None, "row", "col", None, None, None),
        P(None, "row", "col", None),
        P(None, "row", "col"),
        P("row", "col", None, None, None),
    )
    return jax.shard_map(
        per_device,
        mesh=mesh,
        in_specs=placed,
        out_specs=P(None, "row", "col", None, None, None),
        check_vma=False,
    )
```

```python
import functools

import jax
import jax.numpy as jnp
from jax import lax
from jax.experimental import pallas as pl
from jax.experimental.pallas import tpu as pltpu
from jax.sharding import PartitionSpec as P

FAR, OWN_0, OWN_1, NEAR = range(4)
HALF = 32
ZERO = 3 * HALF
INFO = 16
VMEM_LIMIT = 24 * 1024 * 1024


def ring(count, step):
    return [(i, (i + step) % count) for i in range(count)]


def pair(count):
    return [(i, i ^ 1) for i in range(count)]


def outward(count):
    return [(i, (i + (1 if i % 2 else -1)) % count) for i in range(count)]


def aside(count):
    return [(i, (i + (2 if i % 2 else -2)) % count) for i in range(count)]


def onward(count):
    return [(i, (i + (-2 if i % 2 else 2)) % count) for i in range(count)]


def table_kernel(operators, odd_ref, own_1, own_0, joined, table):
    odd = odd_ref[0]
    each = 2 * operators
    wide = table.shape[1] // 9 + 1
    last = joined.shape[0]
    parts = (
        joined[last - INFO :, :],
        own_0[own_0.shape[0] - INFO :, :],
        own_1[own_1.shape[0] - INFO :, :],
        joined[last - 2 * INFO : last - INFO, :],
    )
    info = jnp.concatenate([part.astype(jnp.float32)[:each, :wide] for part in parts], axis=0).astype(jnp.int32)
    slots = info.shape[1] - 1
    shape = table.shape
    row = lax.broadcasted_iota(jnp.int32, shape, 0)
    place = lax.broadcasted_iota(jnp.int32, shape, 1)
    slot = place // 9
    band = place - 9 * slot
    band_y = band // 3
    band_x = band - 3 * band_y
    fine_x = row & 1
    fine_y = row // each - 1
    off = jnp.zeros(shape, jnp.int32)
    for k in range(slots):
        off = off + jnp.where(slot == k, info[:, k : k + 1], 0)
    off_x = jnp.where(off >= 6, 2, jnp.where(off >= 3, 1, 0))
    near_x = fine_x + off_x - 1
    near_y = fine_y + (off - 3 * off_x - 1) * (1 - 2 * odd)
    place_x = band_x - (((near_x - 1) >> 1) - (fine_x >> 1) + 1)
    place_y = band_y - (((near_y - 1) >> 1) - (fine_y >> 1) + 1)
    corner_x = jnp.where((near_x & 1) == 1, place_x, 1 - place_x)
    corner_y = jnp.where((near_y & 1) == 1, place_y, 1 - place_y)
    good = (place_x >= 0) & (place_x < 2) & (place_y >= 0) & (place_y < 2)
    good = good & (slot < info[:, slots:])
    side = jnp.where(near_y < 0, 2 * HALF, jnp.where(near_y < 2, 0, HALF))
    index = side + (near_x + 1) * 8 + ((near_y & 1) ^ odd) * 4 + 2 * corner_x + corner_y
    table[...] = jnp.where(good, index, ZERO)


def table_row(operators, role, operator, x):
    return (role * operators + operator) * 2 + x


def fill(flat, first, low, mid, high):
    for piece, start in ((low, 0), (mid, 8), (high, 24)):
        for x in range(piece.shape[0]):
            for y in range(2):
                flat[pl.ds(first + start + 8 * x + 4 * y, 4)] = piece[x, y]


def pack_kernel(odd_ref, off, count, a_own, *outs):
    operators, _, _, slots = off.shape
    block = a_own.shape[-1]
    odd = odd_ref[0]
    row = lax.broadcasted_iota(jnp.int32, (INFO, block), 0)
    lane = lax.broadcasted_iota(jnp.int32, (INFO, block), 1)
    for out, y in zip(outs, (1 - odd, odd)):
        for x in range(2):
            for k in range(slots):
                out[pl.ds((x * slots + k) * block, block), :] = a_own[0, x, y, k]
        line = jnp.zeros((INFO, block), jnp.int32)
        for s in range(operators):
            for x in range(2):
                here = row == 2 * s + x
                line = jnp.where(here & (lane == slots), count[s, x, y], line)
                for k in range(slots):
                    line = jnp.where(here & (lane == k), off[s, x, y, k], line)
        out[pl.ds(2 * slots * block, INFO), :] = line.astype(jnp.float32).astype(out.dtype)
    for s in range(1, operators):
        for out, y in zip(outs[2 * s : 2 * s + 2], (1 - odd, odd)):
            for x in range(2):
                out[x, 0] = a_own[s, x, y]


def rows_kernel(own, near, low, high):
    for out, x in ((low, 0), (high, 1)):
        out[0, 0:2] = own[x]
        out[0, 2:4] = near[x]


def join_kernel(near, far, out):
    count = near.shape[0] - INFO
    out[pl.ds(0, count), :] = near[pl.ds(0, count), :]
    out[pl.ds(count, count), :] = far[pl.ds(0, count), :]
    out[pl.ds(2 * count, INFO), :] = near[pl.ds(count, INFO), :]
    out[pl.ds(2 * count + INFO, INFO), :] = far[pl.ds(count, INFO), :]


def joined_row(joined, side, x):
    block = joined.shape[1]
    slots = joined.shape[0] // (4 * block)
    first = (side * 2 + x) * slots
    return [joined.at[pl.ds((first + k) * block, block), :] for k in range(slots)]


def row_of(array):
    return [array.at[k] for k in range(array.shape[0])]


def fine_row(table, number, flat, blocks, w_ref):
    slots = len(blocks)
    left = jnp.concatenate([ref[...] for ref in blocks], axis=1)
    for band_y in range(3):
        right = jnp.concatenate(
            [
                jnp.concatenate(
                    [flat[table[number, k * 9 + band_y * 3 + band_x]] for band_x in range(3)], axis=1
                )
                for k in range(slots)
            ],
            axis=0,
        )
        w_ref[band_y] = jnp.dot(left, right, preferred_element_type=jnp.float32).astype(w_ref.dtype)


def coarse_column(odd, pieces, w_refs, fine_rows, lag_y, corner_x):
    lefts, rights = [], []
    for fine_x in fine_rows:
        for role in range(4):
            fine_y = role - 1
            band_y = lag_y - (fine_y // 2 + 1)
            if 0 <= band_y < 3:
                corner_y = 1 if role in (FAR, NEAR) else 0
                lefts.append(pieces[role][fine_x, (fine_y & 1) ^ odd, corner_x + corner_y])
                rights.append(w_refs[role][fine_x, band_y])
    left = jnp.concatenate(lefts, axis=0)
    right = jnp.concatenate(rights, axis=0)
    return lax.dot_general(left, right, (((0,), (0,)), ((), ())), preferred_element_type=jnp.float32)


def edges(odd, pieces, w_refs, outs):
    block = outs[0].shape[-1]
    for fine_x, out in enumerate(outs):
        for lag_y in range(5):
            total = coarse_column(odd, pieces, w_refs, (fine_x,), lag_y, 2)
            for lag_x in range(3):
                out[lag_x, lag_y] = total[:, lag_x * block : (lag_x + 1) * block].astype(out.dtype)


def near_own_kernel(operators, table, odd_ref, a_own, p_own, p_near, low, high, flat, w_ref):
    odd = odd_ref[0]
    fill(flat, 0, low.at[:, 0:2], p_own, high.at[:, 0:2])
    fill(flat, HALF, low.at[:, 2:4], p_near, high.at[:, 2:4])
    flat[ZERO] = jnp.zeros(flat.shape[1:], flat.dtype)
    for s in range(operators):
        for x in range(2):
            fine_row(table, table_row(operators, OWN_1, s, x), flat, row_of(a_own.at[s, x, 1 - odd]), w_ref.at[s, x])


def near_kernel(operators, operator, table, flat, a_pair, w_ref):
    for x in range(2):
        fine_row(table, table_row(operators, NEAR, operator, x), flat, joined_row(a_pair, 0, x), w_ref.at[x])


def far_first_kernel(
    operators, table, odd_ref, a_own, a_pair, w_own, w_near, p_own, p_near, p_far, far_low, far_high, held, low, high, flat, w_own_0, w_far
):
    odd = odd_ref[0]
    fill(flat, 2 * HALF, far_low, p_far, far_high)
    for x in range(2):
        fine_row(table, table_row(operators, FAR, 0, x), flat, joined_row(a_pair, 1, x), w_far.at[x])
        fine_row(table, table_row(operators, OWN_0, 0, x), flat, row_of(a_own.at[0, x, odd]), w_own_0.at[x])
    edges(odd, (p_far, p_own, p_own, p_near), (w_far, w_own_0, w_own.at[0], w_near), (low, high))


def own_0_kernel(operators, operator, table, odd_ref, a_own, flat, w_ref):
    odd = odd_ref[0]
    for x in range(2):
        fine_row(table, table_row(operators, OWN_0, operator, x), flat, row_of(a_own.at[operator, x, odd]), w_ref.at[x])


def sides_kernel(
    operators, operator, table, odd_ref, a_near, a_far, flat, w_own, w_own_0, p_own, p_near, p_far, low, high, w_near, w_far
):
    odd = odd_ref[0]
    for x in range(2):
        fine_row(table, table_row(operators, NEAR, operator, x), flat, row_of(a_near.at[x, 0]), w_near.at[x])
        fine_row(table, table_row(operators, FAR, operator, x), flat, row_of(a_far.at[x, 0]), w_far.at[x])
    edges(odd, (p_far, p_own, p_own, p_near), (w_far, w_own_0, w_own.at[operator], w_near), (low, high))


def centre_kernel(operator, odd_ref, p_own, p_near, p_far, w_far, w_own_0, w_own, w_near, out):
    block = out.shape[-1]
    odd = odd_ref[0]
    for lag_y in range(5):
        total = coarse_column(
            odd, (p_far, p_own, p_own, p_near), (w_far, w_own_0, w_own.at[operator], w_near), (0, 1), lag_y, 0
        )
        for lag_x in range(3):
            out[lag_x, lag_y] = total[:, lag_x * block : (lag_x + 1) * block]


def final_kernel(odd_ref, *refs):
    out = refs[-1]
    odd = odd_ref[0]
    for operator in range(out.shape[0]):
        own, low, high = refs[3 * operator : 3 * operator + 3]
        for lag_x in range(5):
            for lag_y in range(5):
                total = None
                for part, first in ((low, 0), (own, 1), (high, 2)):
                    if 0 <= lag_x - first < 3:
                        term = part[lag_x - first, lag_y].astype(jnp.float32)
                        total = term if total is None else total + term
                place = 5 * lag_x + lag_y + odd * (4 - 2 * lag_y)
                out[operator, 0, 0, place] = total.astype(out.dtype)


def per_device(a_vals, a_off, a_count, p_vals):
    operators, _, _, slots, block, _ = a_vals.shape
    cols = lax.axis_size("col")
    rows = lax.axis_size("row")
    odd = (lax.axis_index("col") & 1).astype(jnp.int32)
    up, down = ring(rows, 1), ring(rows, -1)
    near_way, far_way, on_way, aside_way = pair(cols), outward(cols), onward(cols), aside(cols)

    smem = pl.BlockSpec(memory_space=pltpu.SMEM)
    vmem = pl.BlockSpec(memory_space=pltpu.VMEM)
    bf16, f32 = jnp.bfloat16, jnp.float32
    odd_arg = odd[None]
    flat_shape = jax.ShapeDtypeStruct((ZERO + 1, block, block), bf16)
    w_shape = jax.ShapeDtypeStruct((2, 3, block, 3 * block), bf16)
    part_shape = jax.ShapeDtypeStruct((3, 5, block, block), bf16)

    def call(kernel, in_specs, out_shape, products, name, scratch=(), aliases=None, limit=VMEM_LIMIT):
        single = not isinstance(out_shape, list)
        return pl.pallas_call(
            kernel,
            in_specs=in_specs,
            out_specs=vmem if single else [vmem] * len(out_shape),
            out_shape=out_shape,
            scratch_shapes=list(scratch),
            input_output_aliases=aliases or {},
            compiler_params=pltpu.CompilerParams(vmem_limit_bytes=limit),
            cost_estimate=pl.CostEstimate(flops=products, bytes_accessed=1024, transcendentals=0),
            name=name,
        )

    p_near = lax.ppermute(p_vals, "col", near_way)
    column = jax.ShapeDtypeStruct((2 * slots * block + INFO, block), bf16)
    later = jax.ShapeDtypeStruct((2, 1, slots, block, block), bf16)
    own_1, own_0, *later = call(
        pack_kernel, [smem] * 3 + [vmem], [column] * 2 + [later] * (2 * operators - 2), 1, "pack"
    )(odd_arg, a_off, a_count, a_vals)
    moved = lax.ppermute(own_0, "col", aside_way)
    joined = jax.ShapeDtypeStruct((4 * slots * block + 2 * INFO, block), bf16)
    joined = call(join_kernel, [vmem, vmem], joined, 1, "join")(own_1, moved)
    p_near, joined = lax.optimization_barrier((p_near, joined))
    p_far = lax.ppermute(p_near, "col", on_way)
    from_pair = lax.ppermute(joined, "col", near_way)
    a_near, a_far = [None], [None]
    row_shape = jax.ShapeDtypeStruct((1, 4, 4, block, block), bf16)
    low, high = call(rows_kernel, [vmem, vmem], [row_shape, row_shape], 1, "rows")(p_vals, p_near)
    from_low = lax.ppermute(high, "row", up)
    from_high = lax.ppermute(low, "row", down)
    table = call(
        functools.partial(table_kernel, operators),
        [smem] + [vmem] * 3,
        jax.ShapeDtypeStruct((operators * 8, slots * 9), jnp.int32),
        1,
        "table",
    )(odd_arg, own_1, own_0, from_pair)
    from_pair, later = lax.optimization_barrier((from_pair, later))
    far_low = lax.ppermute(p_far[1:2], "row", up)
    far_high = lax.ppermute(p_far[0:1], "row", down)
    a_near += [lax.ppermute(send, "col", near_way) for send in later[0::2]]
    a_far += [lax.ppermute(send, "col", far_way) for send in later[1::2]]

    flat, w_own = call(
        functools.partial(near_own_kernel, operators),
        [smem, smem] + [vmem] * 5,
        [flat_shape, jax.ShapeDtypeStruct((operators,) + w_shape.shape, bf16)],
        360,
        "near_own",
    )(table, odd_arg, a_vals, p_vals, p_near, from_low, from_high)

    finals = []
    for s in range(operators):
        if s == 0:
            w_near = call(functools.partial(near_kernel, operators, s), [smem, vmem, vmem], w_shape, 90, "near")(
                table, flat, from_pair
            )
            low, high, flat, w_own_0, w_far = call(
                functools.partial(far_first_kernel, operators),
                [smem, smem] + [vmem] * 10,
                [part_shape, part_shape, flat_shape, w_shape, w_shape],
                300,
                "far_first",
                aliases={11: 2},
            )(table, odd_arg, a_vals, from_pair, w_own, w_near, p_vals, p_near, p_far, far_low, far_high, flat)
        else:
            w_own_0 = call(functools.partial(own_0_kernel, operators, s), [smem, smem, vmem, vmem], w_shape, 90, "own_0")(
                table, odd_arg, a_vals, flat
            )
            low, high, w_near, w_far = call(
                functools.partial(sides_kernel, operators, s),
                [smem, smem] + [vmem] * 8,
                [part_shape, part_shape, w_shape, w_shape],
                200,
                "sides",
            )(table, odd_arg, a_near[s], a_far[s], flat, w_own, w_own_0, p_vals, p_near, p_far)
        from_low = lax.ppermute(high, "row", up)
        from_high = lax.ppermute(low, "row", down)
        centre = call(
            functools.partial(centre_kernel, s),
            [smem] + [vmem] * 7,
            jax.ShapeDtypeStruct((3, 5, block, block), f32),
            144,
            "centre",
        )(odd_arg, p_vals, p_near, p_far, w_far, w_own_0, w_own, w_near)
        finals += [centre, from_low, from_high]
    return call(
        final_kernel,
        [smem] + [vmem] * len(finals),
        jax.ShapeDtypeStruct((operators, 1, 1, 25, block, block), bf16),
        1,
        "final",
    )(odd_arg, *finals)


def solution(mesh):
    placed = (
        P(None, "row", "col", None, None, None),
        P(None, "row", "col", None),
        P(None, "row", "col"),
        P("row", "col", None, None, None),
    )
    return jax.shard_map(
        per_device,
        mesh=mesh,
        in_specs=placed,
        out_specs=P(None, "row", "col", None, None, None),
        check_vma=False,
    )
```

```python
import functools

import jax
import jax.numpy as jnp
from jax import lax
from jax.experimental import pallas as pl
from jax.experimental.pallas import tpu as pltpu
from jax.sharding import PartitionSpec as P

FAR, OWN_0, OWN_1, NEAR = range(4)
HALF = 32
ZERO = 3 * HALF
INFO = 16
LONG = 10**11
VMEM_LIMIT = 24 * 1024 * 1024


def pair(count):
    return [(i, i ^ 1) for i in range(count)]


def outward(count):
    return [(i, (i + (1 if i % 2 else -1)) % count) for i in range(count)]


def aside(count):
    return [(i, (i + (2 if i % 2 else -2)) % count) for i in range(count)]


def onward(count):
    return [(i, (i + (-2 if i % 2 else 2)) % count) for i in range(count)]


def table_kernel(operators, roles, turn, *refs):
    table = refs[-1]
    odd, flip = turns(turn)
    each = 2 * operators
    wide = table.shape[1] // 9 + 1
    parts = []
    for place in range(2):
        array = refs[min(place, len(refs) - 2)]
        last = array.shape[0] - (INFO if len(refs) == 2 and place == 0 else 0)
        parts.append(array[last - INFO : last, :].astype(jnp.float32)[:each, :wide])
    info = jnp.concatenate(parts, axis=0).astype(jnp.int32)
    slots = info.shape[1] - 1
    shape = table.shape
    row = lax.broadcasted_iota(jnp.int32, shape, 0)
    place = lax.broadcasted_iota(jnp.int32, shape, 1)
    slot = place // 9
    band = place - 9 * slot
    band_y = band // 3
    band_x = band - 3 * band_y
    fine_x = row & 1
    fine_y = jnp.where(row < each, roles[0], roles[1]) - 1
    off = jnp.zeros(shape, jnp.int32)
    for k in range(slots):
        off = off + jnp.where(slot == k, info[:, k : k + 1], 0)
    off_x = jnp.where(off >= 6, 2, jnp.where(off >= 3, 1, 0))
    near_x = fine_x + (off_x - 1) * (1 - 2 * flip)
    near_y = fine_y + (off - 3 * off_x - 1) * (1 - 2 * odd)
    place_x = band_x - (((near_x - 1) >> 1) - (fine_x >> 1) + 1)
    place_y = band_y - (((near_y - 1) >> 1) - (fine_y >> 1) + 1)
    corner_x = jnp.where((near_x & 1) == 1, place_x, 1 - place_x)
    corner_y = jnp.where((near_y & 1) == 1, place_y, 1 - place_y)
    good = (place_x >= 0) & (place_x < 2) & (place_y >= 0) & (place_y < 2)
    good = good & (slot < info[:, slots:])
    side = jnp.where(near_y < 0, 2 * HALF, jnp.where(near_y < 2, 0, HALF))
    index = side + (near_x + 1) * 8 + ((near_y & 1) ^ odd) * 4 + 2 * corner_x + corner_y
    table[...] = jnp.where(good, index, ZERO)


def table_row(operators, role, operator, x):
    return (operators if role in (OWN_1, FAR) else 0) * 2 + operator * 2 + x


def turns(turn):
    return turn[0] & 1, turn[0] >> 1


def fill(flat, first, rows):
    for x, piece, at in rows:
        for y in range(2):
            flat[pl.ds(first + 8 * (x + 1) + 4 * y, 4)] = piece[at, y]


def rows_kernel(turn, piece, *outs):
    flip = turns(turn)[1]
    for out, x in zip(outs, (1 - flip, flip)):
        out[0] = piece[x]


def pack_kernel(turn, off, count, a_own, *outs):
    operators, _, _, slots = off.shape
    block = a_own.shape[-1]
    odd, flip = turns(turn)
    row = lax.broadcasted_iota(jnp.int32, (INFO, block), 0)
    lane = lax.broadcasted_iota(jnp.int32, (INFO, block), 1)
    for out, y in zip(outs, (1 - odd, odd)):
        for x in range(2):
            for k in range(slots):
                out[pl.ds((x * slots + k) * block, block), :] = a_own[0, x ^ flip, y, k]
        line = jnp.zeros((INFO, block), jnp.int32)
        for s in range(operators):
            for x in range(2):
                here = row == 2 * s + x
                line = jnp.where(here & (lane == slots), count[s, x ^ flip, y], line)
                for k in range(slots):
                    line = jnp.where(here & (lane == k), off[s, x ^ flip, y, k], line)
        out[pl.ds(2 * slots * block, INFO), :] = line.astype(jnp.float32).astype(out.dtype)


def later_kernel(turn, a_own, after, *outs):
    odd, flip = turns(turn)
    for i, out in enumerate(outs):
        for x in range(2):
            out[x, 0] = a_own[i // 2 + 1, x ^ flip, odd if i % 2 else 1 - odd]


def join_kernel(near, far, out):
    count = near.shape[0] - INFO
    out[pl.ds(0, count), :] = near[pl.ds(0, count), :]
    out[pl.ds(count, count), :] = far[pl.ds(0, count), :]
    out[pl.ds(2 * count, INFO), :] = near[pl.ds(count, INFO), :]
    out[pl.ds(2 * count + INFO, INFO), :] = far[pl.ds(count, INFO), :]


def joined_row(joined, side, x):
    block = joined.shape[1]
    slots = joined.shape[0] // (4 * block)
    first = (side * 2 + x) * slots
    return [joined.at[pl.ds((first + k) * block, block), :] for k in range(slots)]


def row_of(array):
    return [array.at[k] for k in range(array.shape[0])]


def fine_row(table, number, flat, blocks, w_ref):
    slots = len(blocks)
    left = jnp.concatenate([ref[...] for ref in blocks], axis=1)
    for band_y in range(3):
        right = jnp.concatenate(
            [
                jnp.concatenate(
                    [flat[table[number, k * 9 + band_y * 3 + band_x]] for band_x in range(3)], axis=1
                )
                for k in range(slots)
            ],
            axis=0,
        )
        w_ref[band_y] = jnp.dot(left, right, preferred_element_type=jnp.float32).astype(w_ref.dtype)


def coarse_column(turn, pieces, w_refs, fine_rows, lag_y, corner_x):
    odd, flip = turns(turn)
    lefts, rights = [], []
    for fine_x in fine_rows:
        for role in range(4):
            fine_y = role - 1
            band_y = lag_y - (fine_y // 2 + 1)
            if 0 <= band_y < 3:
                corner_y = 1 if role in (FAR, NEAR) else 0
                lefts.append(pieces[role][fine_x ^ flip, (fine_y & 1) ^ odd, corner_x + corner_y])
                rights.append(w_refs[role][fine_x][band_y])
    left = jnp.concatenate(lefts, axis=0)
    right = jnp.concatenate(rights, axis=0)
    return lax.dot_general(left, right, (((0,), (0,)), ((), ())), preferred_element_type=jnp.float32)


def edge(turn, pieces, w_refs, fine_x, out):
    block = out.shape[-1]
    for lag_y in range(5):
        total = coarse_column(turn, pieces, w_refs, (fine_x,), lag_y, 2)
        for lag_x in range(3):
            out[lag_x, lag_y] = total[:, lag_x * block : (lag_x + 1) * block].astype(out.dtype)


def near_own_kernel(operators, table, turn, a_own, p_own, p_near, own_out, own_in, near_out, near_in, flat, w_ref):
    odd, flip = turns(turn)
    fill(flat, 0, ((-1, own_out, 0), (0, p_own, flip), (1, p_own, 1 - flip), (2, own_in, 0)))
    fill(flat, HALF, ((-1, near_out, 0), (0, p_near, flip), (1, p_near, 1 - flip), (2, near_in, 0)))
    flat[ZERO] = jnp.zeros(flat.shape[1:], flat.dtype)
    for s in range(operators):
        for x in range(2):
            fine_row(table, table_row(operators, OWN_1, s, x), flat, row_of(a_own.at[s, x ^ flip, 1 - odd]), w_ref.at[s, x])


def near_kernel(operators, table, flat, a_pair, w_ref):
    fine_row(table, table_row(operators, NEAR, 0, 0), flat, joined_row(a_pair, 0, 0), w_ref)


def first_outer_kernel(
    operators, own_table, table, turn, a_own, a_pair, w_own, w_near, p_own, p_near, p_far, far_out, held, out, flat, w_far, w_own_0
):
    odd, flip = turns(turn)
    fill(flat, 2 * HALF, ((-1, far_out, 0), (0, p_far, flip), (1, p_far, 1 - flip)))
    fine_row(table, table_row(operators, FAR, 0, 0), flat, joined_row(a_pair, 1, 0), w_far)
    fine_row(own_table, table_row(operators, OWN_0, 0, 0), flat, row_of(a_own.at[0, flip, odd]), w_own_0)
    edge(turn, (p_far, p_own, p_own, p_near), one_row(0, w_far, w_own_0, w_own.at[0, 0], w_near), 0, out)


def first_inner_kernel(
    operators, own_table, table, turn, a_own, a_pair, w_own, p_own, p_near, p_far, far_in, held, out, flat, w_far, w_own_0, w_near
):
    odd, flip = turns(turn)
    fill(flat, 2 * HALF, ((2, far_in, 0),))
    fine_row(table, table_row(operators, NEAR, 0, 1), flat, joined_row(a_pair, 0, 1), w_near)
    fine_row(table, table_row(operators, FAR, 0, 1), flat, joined_row(a_pair, 1, 1), w_far)
    fine_row(own_table, table_row(operators, OWN_0, 0, 1), flat, row_of(a_own.at[0, 1 - flip, odd]), w_own_0)
    edge(turn, (p_far, p_own, p_own, p_near), one_row(1, w_far, w_own_0, w_own.at[0, 1], w_near), 1, out)


def one_row(x, *w_refs):
    return [{x: ref} for ref in w_refs]


def own_0_kernel(operators, operator, table, turn, a_own, flat, *w_refs):
    odd, flip = turns(turn)
    for x in range(2):
        fine_row(table, table_row(operators, OWN_0, operator, x), flat, row_of(a_own.at[operator, x ^ flip, odd]), w_refs[x])


def sides_kernel(
    operators, operator, table, turn, a_near, a_far, flat, w_own, own_w_0, own_w_1, p_own, p_near, p_far, outer, inner, *w_refs
):
    for x, (out, w_own_0) in enumerate(((outer, own_w_0), (inner, own_w_1))):
        w_near, w_far = w_refs[2 * x : 2 * x + 2]
        fine_row(table, table_row(operators, NEAR, operator, x), flat, row_of(a_near.at[x, 0]), w_near)
        fine_row(table, table_row(operators, FAR, operator, x), flat, row_of(a_far.at[x, 0]), w_far)
        edge(turn, (p_far, p_own, p_own, p_near), one_row(x, w_far, w_own_0, w_own.at[operator, x], w_near), x, out)


def centre_kernel(operator, turn, p_own, p_near, p_far, w_own, *refs):
    out = refs[-1]
    block = out.shape[-1]
    w_refs = (refs[0:2], refs[2:4], (w_own.at[operator, 0], w_own.at[operator, 1]), refs[4:6])
    for lag_y in range(5):
        total = coarse_column(turn, (p_far, p_own, p_own, p_near), w_refs, (0, 1), lag_y, 0)
        for lag_x in range(3):
            out[lag_x, lag_y] = total[:, lag_x * block : (lag_x + 1) * block]


def final_kernel(turn, *refs):
    out = refs[-1]
    odd, flip = turns(turn)
    for operator in range(out.shape[0]):
        own, outer, inner = refs[3 * operator : 3 * operator + 3]
        for lag_x in range(5):
            for lag_y in range(5):
                total = None
                for part, at in ((outer, 2 - lag_x), (own, lag_x - 1), (inner, 4 - lag_x)):
                    if 0 <= at < 3:
                        term = part[at, lag_y].astype(jnp.float32)
                        total = term if total is None else total + term
                place = 5 * (lag_x + flip * (4 - 2 * lag_x)) + lag_y + odd * (4 - 2 * lag_y)
                out[operator, 0, 0, place] = total.astype(out.dtype)


def per_device(a_vals, a_off, a_count, p_vals):
    operators, _, _, slots, block, _ = a_vals.shape
    cols = lax.axis_size("col")
    rows = lax.axis_size("row")
    odd = (lax.axis_index("col") & 1).astype(jnp.int32)
    flip = (lax.axis_index("row") & 1).astype(jnp.int32)
    in_way, out_way = pair(rows), outward(rows)
    near_way, far_way, on_way, aside_way = pair(cols), outward(cols), onward(cols), aside(cols)

    smem = pl.BlockSpec(memory_space=pltpu.SMEM)
    any_spec = pl.BlockSpec(memory_space=pl.ANY)
    vmem = pl.BlockSpec(memory_space=pltpu.VMEM)
    bf16, f32 = jnp.bfloat16, jnp.float32
    turn = (odd + 2 * flip)[None]
    flat_shape = jax.ShapeDtypeStruct((ZERO + 1, block, block), bf16)
    w_shape = jax.ShapeDtypeStruct((3, block, 3 * block), bf16)
    part_shape = jax.ShapeDtypeStruct((3, 5, block, block), bf16)

    def call(kernel, in_specs, out_shape, products, name, scratch=(), aliases=None, limit=VMEM_LIMIT):
        single = not isinstance(out_shape, list)
        return pl.pallas_call(
            kernel,
            in_specs=in_specs,
            out_specs=vmem if single else [vmem] * len(out_shape),
            out_shape=out_shape,
            scratch_shapes=list(scratch),
            input_output_aliases=aliases or {},
            compiler_params=pltpu.CompilerParams(vmem_limit_bytes=limit),
            cost_estimate=pl.CostEstimate(flops=products, bytes_accessed=1024, transcendentals=0),
            name=name,
        )

    p_near = lax.ppermute(p_vals, "col", near_way)
    column = jax.ShapeDtypeStruct((2 * slots * block + INFO, block), bf16)
    own_1, own_0 = call(pack_kernel, [smem] * 3 + [vmem], [column] * 2, 1, "pack")(turn, a_off, a_count, a_vals)
    moved = lax.ppermute(own_0, "col", aside_way)
    table_shape = jax.ShapeDtypeStruct((operators * 4, slots * 9), jnp.int32)
    own_table = call(
        functools.partial(table_kernel, operators, (OWN_0, OWN_1)), [smem, vmem, vmem], table_shape, 1, "own_table"
    )(turn, own_0, own_1)
    joined = jax.ShapeDtypeStruct((4 * slots * block + 2 * INFO, block), bf16)
    joined = call(join_kernel, [vmem, vmem], joined, 1, "join")(own_1, moved)
    row_shape = jax.ShapeDtypeStruct((1, 2, 4, block, block), bf16)
    rows_of = call(rows_kernel, [smem, vmem], [row_shape] * 2, 1, "rows")
    own_in, own_out = rows_of(turn, p_vals)
    own_in = lax.ppermute(own_in, "row", in_way)
    own_out = lax.ppermute(own_out, "row", out_way)
    p_near, joined = lax.optimization_barrier((p_near, joined))
    p_far = lax.ppermute(p_near, "col", on_way)
    from_pair = lax.ppermute(joined, "col", near_way)
    p_rows, own_in, own_out = lax.optimization_barrier((p_near, own_in, own_out))
    near_in, near_out = rows_of(turn, p_rows)
    near_in = lax.ppermute(near_in, "row", in_way)
    near_out = lax.ppermute(near_out, "row", out_way)
    far_out = lax.ppermute(near_out, "col", on_way)
    flat, w_own = call(
        functools.partial(near_own_kernel, operators),
        [smem, smem] + [vmem] * 7,
        [flat_shape, jax.ShapeDtypeStruct((operators, 2) + w_shape.shape, bf16)],
        360,
        "near_own",
    )(own_table, turn, a_vals, p_vals, p_near, own_out, own_in, near_out, near_in)

    p_far, w_own = lax.optimization_barrier((p_far, w_own))
    far_in = call(rows_kernel, [smem, vmem], [row_shape], 1, "row")(turn, p_far)[0]
    later = call(
        later_kernel,
        [smem, vmem, any_spec],
        [jax.ShapeDtypeStruct((2, 1, slots, block, block), bf16)] * (2 * operators - 2),
        1,
        "later",
    )(turn, a_vals, near_in)
    far_in = lax.ppermute(far_in, "row", in_way)
    near_out, later_near = lax.optimization_barrier((near_out, later[0::2]))
    w_own, later_far = lax.optimization_barrier((w_own, later[1::2]))
    side_table = call(
        functools.partial(table_kernel, operators, (NEAR, FAR)), [smem, vmem], table_shape, 1, "side_table"
    )(turn, from_pair)

    near_w = call(functools.partial(near_kernel, operators), [smem, vmem, vmem], w_shape, 45, "near")(
        side_table, flat, from_pair
    )
    a_near, a_far = [None], [None]
    a_near += [lax.ppermute(send, "col", near_way) for send in later_near]
    a_far += [lax.ppermute(send, "col", far_way) for send in later_far]

    finals = []
    for s in range(operators):
        own_w, far_w, sums = [None, None], [None, None], [None, None]
        if s == 0:
            sums[0], flat, far_w[0], own_w[0] = call(
                functools.partial(first_outer_kernel, operators),
                [smem, smem, smem] + [vmem] * 9,
                [part_shape, flat_shape, w_shape, w_shape],
                150,
                "first_outer",
                aliases={11: 1},
            )(own_table, side_table, turn, a_vals, from_pair, w_own, near_w, p_vals, p_near, p_far, far_out, flat)
            sums[1], flat, far_w[1], own_w[1], inner_w = call(
                functools.partial(first_inner_kernel, operators),
                [smem, smem, smem] + [vmem] * 8,
                [part_shape, flat_shape, w_shape, w_shape, w_shape],
                LONG,
                "first_inner",
                aliases={10: 1},
            )(own_table, side_table, turn, a_vals, from_pair, w_own, p_vals, p_near, p_far, far_in, flat)
            near_w = [near_w, inner_w]
        else:
            near_w = [None, None]
            own_w = call(
                functools.partial(own_0_kernel, operators, s), [smem, smem, vmem, vmem], [w_shape] * 2, 90, "own_0"
            )(own_table, turn, a_vals, flat)
            *sums, near_w[0], far_w[0], near_w[1], far_w[1] = call(
                functools.partial(sides_kernel, operators, s),
                [smem, smem] + [vmem] * 9,
                [part_shape] * 2 + [w_shape] * 4,
                200,
                "sides",
            )(side_table, turn, a_near[s], a_far[s], flat, w_own, *own_w, p_vals, p_near, p_far)
        from_out = lax.ppermute(sums[0], "row", out_way)
        from_in = lax.ppermute(sums[1], "row", in_way)
        centre = call(
            functools.partial(centre_kernel, s),
            [smem] + [vmem] * 10,
            jax.ShapeDtypeStruct((3, 5, block, block), f32),
            144,
            "centre",
        )(turn, p_vals, p_near, p_far, w_own, *far_w, *own_w, *near_w)
        finals += [centre, from_out, from_in]
    return call(
        final_kernel,
        [smem] + [vmem] * len(finals),
        jax.ShapeDtypeStruct((operators, 1, 1, 25, block, block), bf16),
        1,
        "final",
    )(turn, *finals)


def solution(mesh):
    placed = (
        P(None, "row", "col", None, None, None),
        P(None, "row", "col", None),
        P(None, "row", "col"),
        P("row", "col", None, None, None),
    )
    return jax.shard_map(
        per_device,
        mesh=mesh,
        in_specs=placed,
        out_specs=P(None, "row", "col", None, None, None),
        check_vma=False,
    )
```

```python
import functools

import jax
import jax.numpy as jnp
from jax import lax
from jax.experimental import pallas as pl
from jax.experimental.pallas import tpu as pltpu
from jax.sharding import PartitionSpec as P

FAR, OWN_0, OWN_1, NEAR = range(4)
HALF = 32
ZERO = 3 * HALF
INFO = 16
LONG = 10**11
VMEM_LIMIT = 24 * 1024 * 1024


def pair(count):
    return [(i, i ^ 1) for i in range(count)]


def outward(count):
    return [(i, (i + (1 if i % 2 else -1)) % count) for i in range(count)]


def aside(count):
    return [(i, (i + (2 if i % 2 else -2)) % count) for i in range(count)]


def onward(count):
    return [(i, (i + (-2 if i % 2 else 2)) % count) for i in range(count)]


def table_kernel(operators, roles, turn, *refs):
    table = refs[-1]
    odd, flip = turns(turn)
    each = 2 * operators
    wide = table.shape[1] // 9 + 1
    parts = []
    for place in range(2):
        array = refs[min(place, len(refs) - 2)]
        last = array.shape[0] - (INFO if len(refs) == 2 and place == 0 else 0)
        parts.append(array[last - INFO : last, :].astype(jnp.float32)[:each, :wide])
    info = jnp.concatenate(parts, axis=0).astype(jnp.int32)
    slots = info.shape[1] - 1
    shape = table.shape
    row = lax.broadcasted_iota(jnp.int32, shape, 0)
    place = lax.broadcasted_iota(jnp.int32, shape, 1)
    slot = place // 9
    band = place - 9 * slot
    band_y = band // 3
    band_x = band - 3 * band_y
    fine_x = row & 1
    fine_y = jnp.where(row < each, roles[0], roles[1]) - 1
    off = jnp.zeros(shape, jnp.int32)
    for k in range(slots):
        off = off + jnp.where(slot == k, info[:, k : k + 1], 0)
    off_x = jnp.where(off >= 6, 2, jnp.where(off >= 3, 1, 0))
    near_x = fine_x + (off_x - 1) * (1 - 2 * flip)
    near_y = fine_y + (off - 3 * off_x - 1) * (1 - 2 * odd)
    place_x = band_x - (((near_x - 1) >> 1) - (fine_x >> 1) + 1)
    place_y = band_y - (((near_y - 1) >> 1) - (fine_y >> 1) + 1)
    corner_x = jnp.where((near_x & 1) == 1, place_x, 1 - place_x)
    corner_y = jnp.where((near_y & 1) == 1, place_y, 1 - place_y)
    good = (place_x >= 0) & (place_x < 2) & (place_y >= 0) & (place_y < 2)
    good = good & (slot < info[:, slots:])
    side = jnp.where(near_y < 0, 2 * HALF, jnp.where(near_y < 2, 0, HALF))
    index = side + (near_x + 1) * 8 + ((near_y & 1) ^ odd) * 4 + 2 * corner_x + corner_y
    table[...] = jnp.where(good, index, ZERO)


def table_row(operators, role, operator, x):
    return (operators if role in (OWN_1, FAR) else 0) * 2 + operator * 2 + x


def turns(turn):
    return turn[0] & 1, turn[0] >> 1


def fill(flat, first, rows):
    for x, piece, at in rows:
        for y in range(2):
            flat[pl.ds(first + 8 * (x + 1) + 4 * y, 4)] = piece[at, y]


def rows_kernel(turn, piece, *outs):
    flip = turns(turn)[1]
    for out, x in zip(outs, (1 - flip, flip)):
        out[0] = piece[x]


def pack_kernel(turn, off, count, a_own, *outs):
    operators, _, _, slots = off.shape
    block = a_own.shape[-1]
    odd, flip = turns(turn)
    row = lax.broadcasted_iota(jnp.int32, (INFO, block), 0)
    lane = lax.broadcasted_iota(jnp.int32, (INFO, block), 1)
    for out, y in zip(outs, (1 - odd, odd)):
        for x in range(2):
            for k in range(slots):
                out[pl.ds((x * slots + k) * block, block), :] = a_own[0, x ^ flip, y, k]
        line = jnp.zeros((INFO, block), jnp.int32)
        for s in range(operators):
            for x in range(2):
                here = row == 2 * s + x
                line = jnp.where(here & (lane == slots), count[s, x ^ flip, y], line)
                for k in range(slots):
                    line = jnp.where(here & (lane == k), off[s, x ^ flip, y, k], line)
        out[pl.ds(2 * slots * block, INFO), :] = line.astype(jnp.float32).astype(out.dtype)


def later_kernel(turn, a_own, after, *outs):
    odd, flip = turns(turn)
    for i, out in enumerate(outs):
        out[...] = a_own[i // 4 + 1, (i // 2 & 1) ^ flip, odd if i % 2 else 1 - odd]


def join_kernel(near, far, out):
    count = near.shape[0] - INFO
    out[pl.ds(0, count), :] = near[pl.ds(0, count), :]
    out[pl.ds(count, count), :] = far[pl.ds(0, count), :]
    out[pl.ds(2 * count, INFO), :] = near[pl.ds(count, INFO), :]
    out[pl.ds(2 * count + INFO, INFO), :] = far[pl.ds(count, INFO), :]


def joined_row(joined, side, x):
    block = joined.shape[1]
    slots = joined.shape[0] // (4 * block)
    first = (side * 2 + x) * slots
    return [joined.at[pl.ds((first + k) * block, block), :] for k in range(slots)]


def row_of(array):
    return [array.at[k] for k in range(array.shape[0])]


def fine_row(table, number, flat, blocks, w_ref):
    slots = len(blocks)
    left = jnp.concatenate([ref[...] for ref in blocks], axis=1)
    for band_y in range(3):
        right = jnp.concatenate(
            [
                jnp.concatenate(
                    [flat[table[number, k * 9 + band_y * 3 + band_x]] for band_x in range(3)], axis=1
                )
                for k in range(slots)
            ],
            axis=0,
        )
        w_ref[band_y] = jnp.dot(left, right, preferred_element_type=jnp.float32).astype(w_ref.dtype)


def coarse_column(turn, pieces, w_refs, fine_rows, lag_y, corner_x):
    odd, flip = turns(turn)
    lefts, rights = [], []
    for fine_x in fine_rows:
        for role in range(4):
            fine_y = role - 1
            band_y = lag_y - (fine_y // 2 + 1)
            if 0 <= band_y < 3:
                corner_y = 1 if role in (FAR, NEAR) else 0
                lefts.append(pieces[role][fine_x ^ flip, (fine_y & 1) ^ odd, corner_x + corner_y])
                rights.append(w_refs[role][fine_x][band_y])
    left = jnp.concatenate(lefts, axis=0)
    right = jnp.concatenate(rights, axis=0)
    return lax.dot_general(left, right, (((0,), (0,)), ((), ())), preferred_element_type=jnp.float32)


def edge(turn, pieces, w_refs, fine_x, out):
    block = out.shape[-1]
    for lag_y in range(5):
        total = coarse_column(turn, pieces, w_refs, (fine_x,), lag_y, 2)
        for lag_x in range(3):
            out[lag_x, lag_y] = total[:, lag_x * block : (lag_x + 1) * block].astype(out.dtype)


def near_own_inner_kernel(operators, table, turn, a_own, p_own, p_near, own_in, near_in, flat, *w_refs):
    odd, flip = turns(turn)
    fill(flat, 0, ((0, p_own, flip), (1, p_own, 1 - flip), (2, own_in, 0)))
    fill(flat, HALF, ((0, p_near, flip), (1, p_near, 1 - flip), (2, near_in, 0)))
    flat[ZERO] = jnp.zeros(flat.shape[1:], flat.dtype)
    for s, w_ref in enumerate(w_refs):
        fine_row(table, table_row(operators, OWN_1, s, 1), flat, row_of(a_own.at[s, 1 - flip, 1 - odd]), w_ref)


def near_own_outer_kernel(operators, table, turn, a_own, own_out, near_out, held, flat, *w_refs):
    odd, flip = turns(turn)
    fill(flat, 0, ((-1, own_out, 0),))
    fill(flat, HALF, ((-1, near_out, 0),))
    for s, w_ref in enumerate(w_refs):
        fine_row(table, table_row(operators, OWN_1, s, 0), flat, row_of(a_own.at[s, flip, 1 - odd]), w_ref)


def near_kernel(operators, table, flat, a_pair, w_ref):
    fine_row(table, table_row(operators, NEAR, 0, 0), flat, joined_row(a_pair, 0, 0), w_ref)


def first_outer_kernel(
    operators, own_table, table, turn, a_own, a_pair, w_own, w_near, p_own, p_near, p_far, far_out, held, out, flat, w_far, w_own_0
):
    odd, flip = turns(turn)
    fill(flat, 2 * HALF, ((-1, far_out, 0), (0, p_far, flip), (1, p_far, 1 - flip)))
    fine_row(table, table_row(operators, FAR, 0, 0), flat, joined_row(a_pair, 1, 0), w_far)
    fine_row(own_table, table_row(operators, OWN_0, 0, 0), flat, row_of(a_own.at[0, flip, odd]), w_own_0)
    edge(turn, (p_far, p_own, p_own, p_near), one_row(0, w_far, w_own_0, w_own, w_near), 0, out)


def first_inner_kernel(
    operators, own_table, table, turn, a_own, a_pair, w_own, p_own, p_near, p_far, far_in, held, out, flat, w_far, w_own_0, w_near
):
    odd, flip = turns(turn)
    fill(flat, 2 * HALF, ((2, far_in, 0),))
    fine_row(table, table_row(operators, NEAR, 0, 1), flat, joined_row(a_pair, 0, 1), w_near)
    fine_row(table, table_row(operators, FAR, 0, 1), flat, joined_row(a_pair, 1, 1), w_far)
    fine_row(own_table, table_row(operators, OWN_0, 0, 1), flat, row_of(a_own.at[0, 1 - flip, odd]), w_own_0)
    edge(turn, (p_far, p_own, p_own, p_near), one_row(1, w_far, w_own_0, w_own, w_near), 1, out)


def one_row(x, *w_refs):
    return [{x: ref} for ref in w_refs]


def sides_kernel(
    operators, operator, x, own_table, table, turn, a_own, a_near, a_far, flat, w_own, p_own, p_near, p_far, out, w_near, w_far, w_own_0
):
    odd, flip = turns(turn)
    fine_row(own_table, table_row(operators, OWN_0, operator, x), flat, row_of(a_own.at[operator, x ^ flip, odd]), w_own_0)
    fine_row(table, table_row(operators, NEAR, operator, x), flat, row_of(a_near), w_near)
    fine_row(table, table_row(operators, FAR, operator, x), flat, row_of(a_far), w_far)
    edge(turn, (p_far, p_own, p_own, p_near), one_row(x, w_far, w_own_0, w_own, w_near), x, out)


def centre_kernel(turn, p_own, p_near, p_far, *refs):
    out = refs[-1]
    block = out.shape[-1]
    w_refs = (refs[0:2], refs[2:4], refs[4:6], refs[6:8])
    for lag_y in range(5):
        total = coarse_column(turn, (p_far, p_own, p_own, p_near), w_refs, (0, 1), lag_y, 0)
        for lag_x in range(3):
            out[lag_x, lag_y] = total[:, lag_x * block : (lag_x + 1) * block]


def final_kernel(operator, turn, own, outer, inner, *refs):
    out, total, sems = refs[-3:]
    odd, flip = turns(turn)
    copies = []
    for lag_x in range(5):
        for lag_y in range(5):
            block = None
            for part, at in ((outer, 2 - lag_x), (own, lag_x - 1), (inner, 4 - lag_x)):
                if 0 <= at < 3:
                    term = part[at, lag_y].astype(jnp.float32)
                    block = term if block is None else block + term
            total[lag_x, lag_y + odd * (4 - 2 * lag_y)] = block.astype(out.dtype)
        place = pl.ds(5 * (lag_x + flip * (4 - 2 * lag_x)), 5)
        copies.append(pltpu.make_async_copy(total.at[lag_x], out.at[operator, 0, 0, place], sems.at[lag_x]))
        copies[-1].start()
    for copy in copies:
        copy.wait()


def per_device(a_vals, a_off, a_count, p_vals):
    operators, _, _, slots, block, _ = a_vals.shape
    cols = lax.axis_size("col")
    rows = lax.axis_size("row")
    odd = (lax.axis_index("col") & 1).astype(jnp.int32)
    flip = (lax.axis_index("row") & 1).astype(jnp.int32)
    in_way, out_way = pair(rows), outward(rows)
    near_way, far_way, on_way, aside_way = pair(cols), outward(cols), onward(cols), aside(cols)

    smem = pl.BlockSpec(memory_space=pltpu.SMEM)
    any_spec = pl.BlockSpec(memory_space=pl.ANY)
    vmem = pl.BlockSpec(memory_space=pltpu.VMEM)
    bf16, f32 = jnp.bfloat16, jnp.float32
    turn = (odd + 2 * flip)[None]
    flat_shape = jax.ShapeDtypeStruct((ZERO + 1, block, block), bf16)
    w_shape = jax.ShapeDtypeStruct((3, block, 3 * block), bf16)
    part_shape = jax.ShapeDtypeStruct((3, 5, block, block), bf16)

    def call(kernel, in_specs, out_shape, products, name, scratch=(), aliases=None, limit=VMEM_LIMIT, out_spec=None):
        single = not isinstance(out_shape, list)
        return pl.pallas_call(
            kernel,
            in_specs=in_specs,
            out_specs=(out_spec or vmem) if single else [vmem] * len(out_shape),
            out_shape=out_shape,
            scratch_shapes=list(scratch),
            input_output_aliases=aliases or {},
            compiler_params=pltpu.CompilerParams(vmem_limit_bytes=limit),
            cost_estimate=pl.CostEstimate(flops=products, bytes_accessed=1024, transcendentals=0),
            name=name,
        )

    p_near = lax.ppermute(p_vals, "col", near_way)
    column = jax.ShapeDtypeStruct((2 * slots * block + INFO, block), bf16)
    own_1, own_0 = call(pack_kernel, [smem] * 3 + [vmem], [column] * 2, 1, "pack")(turn, a_off, a_count, a_vals)
    moved = lax.ppermute(own_0, "col", aside_way)
    table_shape = jax.ShapeDtypeStruct((operators * 4, slots * 9), jnp.int32)
    own_table = call(
        functools.partial(table_kernel, operators, (OWN_0, OWN_1)), [smem, vmem, vmem], table_shape, 1, "own_table"
    )(turn, own_0, own_1)
    joined = jax.ShapeDtypeStruct((4 * slots * block + 2 * INFO, block), bf16)
    joined = call(join_kernel, [vmem, vmem], joined, 1, "join")(own_1, moved)
    row_shape = jax.ShapeDtypeStruct((1, 2, 4, block, block), bf16)
    rows_of = call(rows_kernel, [smem, vmem], [row_shape] * 2, 1, "rows")
    own_in, own_out = rows_of(turn, p_vals)
    own_in = lax.ppermute(own_in, "row", in_way)
    own_out = lax.ppermute(own_out, "row", out_way)
    p_near, joined = lax.optimization_barrier((p_near, joined))
    p_far = lax.ppermute(p_near, "col", on_way)
    from_pair = lax.ppermute(joined, "col", near_way)
    p_rows, own_in, own_out = lax.optimization_barrier((p_near, own_in, own_out))
    near_in, near_out = rows_of(turn, p_rows)
    near_in = lax.ppermute(near_in, "row", in_way)
    near_out = lax.ppermute(near_out, "row", out_way)
    far_out = lax.ppermute(near_out, "col", on_way)
    flat, *w_inner = call(
        functools.partial(near_own_inner_kernel, operators),
        [smem, smem] + [vmem] * 5,
        [flat_shape] + [w_shape] * operators,
        180,
        "near_own_inner",
    )(own_table, turn, a_vals, p_vals, p_near, own_in, near_in)
    near_out, flat = lax.optimization_barrier((near_out, flat))
    flat, *w_outer = call(
        functools.partial(near_own_outer_kernel, operators),
        [smem, smem] + [vmem] * 4,
        [flat_shape] + [w_shape] * operators,
        180,
        "near_own_outer",
        aliases={5: 0},
    )(own_table, turn, a_vals, own_out, near_out, flat)
    w_own = [w_outer, w_inner]

    later = call(
        later_kernel,
        [smem, vmem, any_spec],
        [jax.ShapeDtypeStruct((slots, block, block), bf16)] * (4 * operators - 4),
        1,
        "later",
    )(turn, a_vals, own_in)
    side_table = call(
        functools.partial(table_kernel, operators, (NEAR, FAR)), [smem, vmem], table_shape, 1, "side_table"
    )(turn, from_pair)

    near_w = call(functools.partial(near_kernel, operators), [smem, vmem, vmem], w_shape, 45, "near")(
        side_table, flat, from_pair
    )

    near_w, p_far = lax.optimization_barrier((near_w, p_far))
    far_in = call(rows_kernel, [smem, vmem], [row_shape], 1, "row")(turn, p_far)[0]
    far_in = lax.ppermute(far_in, "row", in_way)

    def send_row(x):
        rows_sent = []
        for s in range(1, operators):
            near, far = later[4 * s - 4 + 2 * x : 4 * s - 2 + 2 * x]
            rows_sent.append((lax.ppermute(near, "col", near_way), lax.ppermute(far, "col", far_way)))
        return rows_sent

    w_own, later = lax.optimization_barrier((w_own, later))
    outer_a = send_row(0)

    result = None
    for s in range(operators):
        own_w, far_w, sums = [None, None], [None, None], [None, None]
        if s == 0:
            sums[0], flat, far_w[0], own_w[0] = call(
                functools.partial(first_outer_kernel, operators),
                [smem, smem, smem] + [vmem] * 9,
                [part_shape, flat_shape, w_shape, w_shape],
                LONG,
                "first_outer",
                aliases={11: 1},
            )(own_table, side_table, turn, a_vals, from_pair, w_own[0][0], near_w, p_vals, p_near, p_far, far_out, flat)
            sums[1], flat, far_w[1], own_w[1], inner_w = call(
                functools.partial(first_inner_kernel, operators),
                [smem, smem, smem] + [vmem] * 8,
                [part_shape, flat_shape, w_shape, w_shape, w_shape],
                LONG,
                "first_inner",
                aliases={10: 1},
            )(own_table, side_table, turn, a_vals, from_pair, w_own[1][0], p_vals, p_near, p_far, far_in, flat)
            near_w = [near_w, inner_w]
            inner_w, later = lax.optimization_barrier((inner_w, later))
            a_sides = [None] + list(zip(outer_a, send_row(1)))
        else:
            near_w = [None, None]
            for x in range(2):
                if x == 1:
                    from_out, w_own = lax.optimization_barrier((from_out, w_own))
                sums[x], near_w[x], far_w[x], own_w[x] = call(
                    functools.partial(sides_kernel, operators, s, x),
                    [smem, smem, smem] + [vmem] * 8,
                    [part_shape, w_shape, w_shape, w_shape],
                    100,
                    "sides",
                )(own_table, side_table, turn, a_vals, *a_sides[s][x], flat, w_own[x][s], p_vals, p_near, p_far)
        from_out = lax.ppermute(sums[0], "row", out_way)
        from_in = lax.ppermute(sums[1], "row", in_way)
        centre = call(
            centre_kernel,
            [smem] + [vmem] * 11,
            jax.ShapeDtypeStruct((3, 5, block, block), f32),
            144,
            "centre",
        )(turn, p_vals, p_near, p_far, *far_w, *own_w, w_own[0][s], w_own[1][s], *near_w)
        result = call(
            functools.partial(final_kernel, s),
            [smem] + [vmem] * 3 + ([any_spec] if s else []),
            jax.ShapeDtypeStruct((operators, 1, 1, 25, block, block), bf16),
            1,
            "final",
            [pltpu.VMEM((5, 5, block, block), bf16), pltpu.SemaphoreType.DMA((5,))],
            aliases={4: 0} if s else None,
            out_spec=any_spec,
        )(turn, centre, from_out, from_in, *([result] if s else []))
    return result


def solution(mesh):
    placed = (
        P(None, "row", "col", None, None, None),
        P(None, "row", "col", None),
        P(None, "row", "col"),
        P("row", "col", None, None, None),
    )
    return jax.shard_map(
        per_device,
        mesh=mesh,
        in_specs=placed,
        out_specs=P(None, "row", "col", None, None, None),
        check_vma=False,
    )
```

```python
import functools

import jax
import jax.numpy as jnp
from jax import lax
from jax.experimental import pallas as pl
from jax.experimental.pallas import tpu as pltpu
from jax.sharding import PartitionSpec as P

FAR, OWN_0, OWN_1, NEAR = range(4)
HALF = 32
ZERO = 3 * HALF
INFO = 16
LONG = 10**11
VMEM_LIMIT = 24 * 1024 * 1024


def pair(count):
    return [(i, i ^ 1) for i in range(count)]


def outward(count):
    return [(i, (i + (1 if i % 2 else -1)) % count) for i in range(count)]


def aside(count):
    return [(i, (i + (2 if i % 2 else -2)) % count) for i in range(count)]


def onward(count):
    return [(i, (i + (-2 if i % 2 else 2)) % count) for i in range(count)]


def table_kernel(operators, roles, turn, *refs):
    table = refs[-1]
    odd, flip = turns(turn)
    each = 2 * operators
    wide = table.shape[1] // 9 + 1
    parts = []
    for place in range(2):
        array = refs[min(place, len(refs) - 2)]
        last = array.shape[0] - (INFO if len(refs) == 2 and place == 0 else 0)
        parts.append(array[last - INFO : last, :].astype(jnp.float32)[:each, :wide])
    info = jnp.concatenate(parts, axis=0).astype(jnp.int32)
    slots = info.shape[1] - 1
    shape = table.shape
    row = lax.broadcasted_iota(jnp.int32, shape, 0)
    place = lax.broadcasted_iota(jnp.int32, shape, 1)
    slot = place // 9
    band = place - 9 * slot
    band_y = band // 3
    band_x = band - 3 * band_y
    fine_x = row & 1
    fine_y = jnp.where(row < each, roles[0], roles[1]) - 1
    off = jnp.zeros(shape, jnp.int32)
    for k in range(slots):
        off = off + jnp.where(slot == k, info[:, k : k + 1], 0)
    off_x = jnp.where(off >= 6, 2, jnp.where(off >= 3, 1, 0))
    near_x = fine_x + (off_x - 1) * (1 - 2 * flip)
    near_y = fine_y + (off - 3 * off_x - 1) * (1 - 2 * odd)
    place_x = band_x - (((near_x - 1) >> 1) - (fine_x >> 1) + 1)
    place_y = band_y - (((near_y - 1) >> 1) - (fine_y >> 1) + 1)
    corner_x = jnp.where((near_x & 1) == 1, place_x, 1 - place_x)
    corner_y = jnp.where((near_y & 1) == 1, place_y, 1 - place_y)
    good = (place_x >= 0) & (place_x < 2) & (place_y >= 0) & (place_y < 2)
    good = good & (slot < info[:, slots:])
    side = jnp.where(near_y < 0, 2 * HALF, jnp.where(near_y < 2, 0, HALF))
    index = side + (near_x + 1) * 8 + ((near_y & 1) ^ odd) * 4 + 2 * corner_x + corner_y
    table[...] = jnp.where(good, index, ZERO)


def table_row(operators, role, operator, x):
    return (operators if role in (OWN_1, FAR) else 0) * 2 + operator * 2 + x


def turns(turn):
    return turn[0] & 1, turn[0] >> 1


def fill(flat, first, rows):
    for x, piece, at in rows:
        for y in range(2):
            flat[pl.ds(first + 8 * (x + 1) + 4 * y, 4)] = piece[at, y]


def rows_kernel(turn, piece, *outs):
    flip = turns(turn)[1]
    for out, x in zip(outs, (1 - flip, flip)):
        out[0] = piece[x]


def pack_column(turn, off, count, a_own, y, out):
    operators, _, _, slots = off.shape
    block = a_own.shape[-1]
    flip = turns(turn)[1]
    row = lax.broadcasted_iota(jnp.int32, (INFO, block), 0)
    lane = lax.broadcasted_iota(jnp.int32, (INFO, block), 1)
    for x in range(2):
        for k in range(slots):
            out[pl.ds((x * slots + k) * block, block), :] = a_own[0, x ^ flip, y, k]
    line = jnp.zeros((INFO, block), jnp.int32)
    for s in range(operators):
        for x in range(2):
            here = row == 2 * s + x
            line = jnp.where(here & (lane == slots), count[s, x ^ flip, y], line)
            for k in range(slots):
                line = jnp.where(here & (lane == k), off[s, x ^ flip, y, k], line)
    out[pl.ds(2 * slots * block, INFO), :] = line.astype(jnp.float32).astype(out.dtype)


def pack_far_kernel(turn, off, count, a_own, out):
    pack_column(turn, off, count, a_own, turns(turn)[0], out)


def pack_kernel(turn, off, count, a_own, after, own_1, *later):
    odd, flip = turns(turn)
    for s in range(1, a_own.shape[0]):
        far_0, far_1, near = later[3 * s - 3 : 3 * s]
        for x, far in enumerate((far_0, far_1)):
            far[...] = a_own[s, x ^ flip, odd]
            near[x] = a_own[s, x ^ flip, 1 - odd]
    pack_column(turn, off, count, a_own, 1 - odd, own_1)


def join_kernel(near, far, out):
    count = near.shape[0] - INFO
    out[pl.ds(0, count), :] = near[pl.ds(0, count), :]
    out[pl.ds(count, count), :] = far[pl.ds(0, count), :]
    out[pl.ds(2 * count, INFO), :] = near[pl.ds(count, INFO), :]
    out[pl.ds(2 * count + INFO, INFO), :] = far[pl.ds(count, INFO), :]


def joined_row(joined, side, x):
    block = joined.shape[1]
    slots = joined.shape[0] // (4 * block)
    first = (side * 2 + x) * slots
    return [joined.at[pl.ds((first + k) * block, block), :] for k in range(slots)]


def row_of(array):
    return [array.at[k] for k in range(array.shape[0])]


def fine_row(table, number, flat, blocks, w_ref):
    slots = len(blocks)
    left = jnp.concatenate([ref[...] for ref in blocks], axis=1)
    for band_y in range(3):
        right = jnp.concatenate(
            [
                jnp.concatenate(
                    [flat[table[number, k * 9 + band_y * 3 + band_x]] for band_x in range(3)], axis=1
                )
                for k in range(slots)
            ],
            axis=0,
        )
        w_ref[band_y] = jnp.dot(left, right, preferred_element_type=jnp.float32).astype(w_ref.dtype)


def coarse_column(turn, pieces, w_refs, fine_rows, lag_y, corner_x):
    odd, flip = turns(turn)
    lefts, rights = [], []
    for fine_x in fine_rows:
        for role in range(4):
            fine_y = role - 1
            band_y = lag_y - (fine_y // 2 + 1)
            if 0 <= band_y < 3:
                corner_y = 1 if role in (FAR, NEAR) else 0
                lefts.append(pieces[role][fine_x ^ flip, (fine_y & 1) ^ odd, corner_x + corner_y])
                rights.append(w_refs[role][fine_x][band_y])
    left = jnp.concatenate(lefts, axis=0)
    right = jnp.concatenate(rights, axis=0)
    return lax.dot_general(left, right, (((0,), (0,)), ((), ())), preferred_element_type=jnp.float32)


def edge(turn, pieces, w_refs, fine_x, out):
    block = out.shape[-1]
    for lag_y in range(5):
        total = coarse_column(turn, pieces, w_refs, (fine_x,), lag_y, 2)
        for lag_x in range(3):
            out[lag_x, lag_y] = total[:, lag_x * block : (lag_x + 1) * block].astype(out.dtype)


def near_own_kernel(operators, table, turn, a_own, p_own, p_near, own_out, own_in, near_out, near_in, flat, *w_refs):
    odd, flip = turns(turn)
    fill(flat, 0, ((-1, own_out, 0), (0, p_own, flip), (1, p_own, 1 - flip), (2, own_in, 0)))
    fill(flat, HALF, ((-1, near_out, 0), (0, p_near, flip), (1, p_near, 1 - flip), (2, near_in, 0)))
    flat[ZERO] = jnp.zeros(flat.shape[1:], flat.dtype)
    for s in range(operators):
        for x in range(2):
            fine_row(
                table, table_row(operators, OWN_1, s, x), flat, row_of(a_own.at[s, x ^ flip, 1 - odd]), w_refs[2 * s + x]
            )


def near_kernel(operators, table, flat, a_pair, w_ref):
    fine_row(table, table_row(operators, NEAR, 0, 0), flat, joined_row(a_pair, 0, 0), w_ref)


def first_outer_kernel(
    operators, own_table, table, turn, a_own, a_pair, w_own, w_near, p_own, p_near, p_far, far_out, held, out, flat, w_far, w_own_0
):
    odd, flip = turns(turn)
    fill(flat, 2 * HALF, ((-1, far_out, 0), (0, p_far, flip), (1, p_far, 1 - flip)))
    fine_row(table, table_row(operators, FAR, 0, 0), flat, joined_row(a_pair, 1, 0), w_far)
    fine_row(own_table, table_row(operators, OWN_0, 0, 0), flat, row_of(a_own.at[0, flip, odd]), w_own_0)
    edge(turn, (p_far, p_own, p_own, p_near), one_row(0, w_far, w_own_0, w_own, w_near), 0, out)


def first_inner_kernel(
    operators, own_table, table, turn, a_own, a_pair, w_own, p_own, p_near, p_far, far_in, held, out, flat, w_far, w_own_0, w_near
):
    odd, flip = turns(turn)
    fill(flat, 2 * HALF, ((2, far_in, 0),))
    fine_row(table, table_row(operators, NEAR, 0, 1), flat, joined_row(a_pair, 0, 1), w_near)
    fine_row(table, table_row(operators, FAR, 0, 1), flat, joined_row(a_pair, 1, 1), w_far)
    fine_row(own_table, table_row(operators, OWN_0, 0, 1), flat, row_of(a_own.at[0, 1 - flip, odd]), w_own_0)
    edge(turn, (p_far, p_own, p_own, p_near), one_row(1, w_far, w_own_0, w_own, w_near), 1, out)


def one_row(x, *w_refs):
    return [{x: ref} for ref in w_refs]


def sides_kernel(
    operators, operator, x, own_table, table, turn, a_own, a_near, a_far, flat, w_own, p_own, p_near, p_far, out, w_near, w_far, w_own_0
):
    odd, flip = turns(turn)
    fine_row(own_table, table_row(operators, OWN_0, operator, x), flat, row_of(a_own.at[operator, x ^ flip, odd]), w_own_0)
    fine_row(table, table_row(operators, NEAR, operator, x), flat, row_of(a_near.at[x]), w_near)
    fine_row(table, table_row(operators, FAR, operator, x), flat, row_of(a_far), w_far)
    edge(turn, (p_far, p_own, p_own, p_near), one_row(x, w_far, w_own_0, w_own, w_near), x, out)


def centre_kernel(turn, p_own, p_near, p_far, *refs):
    out = refs[-1]
    block = out.shape[-1]
    w_refs = (refs[0:2], refs[2:4], refs[4:6], refs[6:8])
    for lag_y in range(5):
        total = coarse_column(turn, (p_far, p_own, p_own, p_near), w_refs, (0, 1), lag_y, 0)
        for lag_x in range(3):
            out[lag_x, lag_y] = total[:, lag_x * block : (lag_x + 1) * block]


def final_kernel(operator, turn, own, outer, inner, *refs):
    out, total, sems = refs[-3:]
    odd, flip = turns(turn)
    copies = []
    for lag_x in range(5):
        for lag_y in range(5):
            block = None
            for part, at in ((outer, 2 - lag_x), (own, lag_x - 1), (inner, 4 - lag_x)):
                if 0 <= at < 3:
                    term = part[at, lag_y].astype(jnp.float32)
                    block = term if block is None else block + term
            total[lag_x, lag_y + odd * (4 - 2 * lag_y)] = block.astype(out.dtype)
        place = pl.ds(5 * (lag_x + flip * (4 - 2 * lag_x)), 5)
        copies.append(pltpu.make_async_copy(total.at[lag_x], out.at[operator, 0, 0, place], sems.at[lag_x]))
        copies[-1].start()
    for copy in copies:
        copy.wait()


def per_device(a_vals, a_off, a_count, p_vals):
    operators, _, _, slots, block, _ = a_vals.shape
    cols = lax.axis_size("col")
    rows = lax.axis_size("row")
    odd = (lax.axis_index("col") & 1).astype(jnp.int32)
    flip = (lax.axis_index("row") & 1).astype(jnp.int32)
    in_way, out_way = pair(rows), outward(rows)
    near_way, far_way, on_way, aside_way = pair(cols), outward(cols), onward(cols), aside(cols)

    smem = pl.BlockSpec(memory_space=pltpu.SMEM)
    any_spec = pl.BlockSpec(memory_space=pl.ANY)
    vmem = pl.BlockSpec(memory_space=pltpu.VMEM)
    bf16, f32 = jnp.bfloat16, jnp.float32
    turn = (odd + 2 * flip)[None]
    flat_shape = jax.ShapeDtypeStruct((ZERO + 1, block, block), bf16)
    w_shape = jax.ShapeDtypeStruct((3, block, 3 * block), bf16)
    part_shape = jax.ShapeDtypeStruct((3, 5, block, block), bf16)

    def call(kernel, in_specs, out_shape, products, name, scratch=(), aliases=None, limit=VMEM_LIMIT, out_spec=None):
        single = not isinstance(out_shape, list)
        return pl.pallas_call(
            kernel,
            in_specs=in_specs,
            out_specs=(out_spec or vmem) if single else [vmem] * len(out_shape),
            out_shape=out_shape,
            scratch_shapes=list(scratch),
            input_output_aliases=aliases or {},
            compiler_params=pltpu.CompilerParams(vmem_limit_bytes=limit),
            cost_estimate=pl.CostEstimate(flops=products, bytes_accessed=1024, transcendentals=0),
            name=name,
        )

    p_near = lax.ppermute(p_vals, "col", near_way)
    column = jax.ShapeDtypeStruct((2 * slots * block + INFO, block), bf16)
    slots_shape = jax.ShapeDtypeStruct((slots, block, block), bf16)
    two_slots = jax.ShapeDtypeStruct((2, slots, block, block), bf16)
    own_0 = call(pack_far_kernel, [smem] * 3 + [vmem], column, 1, "pack_far", limit=60 << 20)(
        turn, a_off, a_count, a_vals
    )
    own_1, *later = call(
        pack_kernel, [smem] * 3 + [vmem, any_spec], [column] + [slots_shape, slots_shape, two_slots] * (operators - 1), 1, "pack"
    )(turn, a_off, a_count, a_vals, own_0)
    moved = lax.ppermute(own_0, "col", aside_way)
    table_shape = jax.ShapeDtypeStruct((operators * 4, slots * 9), jnp.int32)
    own_table = call(
        functools.partial(table_kernel, operators, (OWN_0, OWN_1)), [smem, vmem, vmem], table_shape, 1, "own_table"
    )(turn, own_0, own_1)
    joined = jax.ShapeDtypeStruct((4 * slots * block + 2 * INFO, block), bf16)
    joined = call(join_kernel, [vmem, vmem], joined, 1, "join")(own_1, moved)
    row_shape = jax.ShapeDtypeStruct((1, 2, 4, block, block), bf16)
    rows_of = call(rows_kernel, [smem, vmem], [row_shape] * 2, 1, "rows")
    own_in, own_out = rows_of(turn, p_vals)
    own_in = lax.ppermute(own_in, "row", in_way)
    own_out = lax.ppermute(own_out, "row", out_way)
    p_near, joined = lax.optimization_barrier((p_near, joined))
    p_far = lax.ppermute(p_near, "col", on_way)
    from_pair = lax.ppermute(joined, "col", near_way)
    p_rows, own_in, own_out = lax.optimization_barrier((p_near, own_in, own_out))
    near_in, near_out = rows_of(turn, p_rows)
    near_in = lax.ppermute(near_in, "row", in_way)
    near_out = lax.ppermute(near_out, "row", out_way)
    far_out = lax.ppermute(near_out, "col", on_way)
    flat, *w_own = call(
        functools.partial(near_own_kernel, operators),
        [smem, smem] + [vmem] * 7,
        [flat_shape] + [w_shape] * (2 * operators),
        360,
        "near_own",
    )(own_table, turn, a_vals, p_vals, p_near, own_out, own_in, near_out, near_in)
    w_own = [w_own[0::2], w_own[1::2]]

    side_table = call(
        functools.partial(table_kernel, operators, (NEAR, FAR)), [smem, vmem], table_shape, 1, "side_table"
    )(turn, from_pair)

    near_w = call(functools.partial(near_kernel, operators), [smem, vmem, vmem], w_shape, 45, "near")(
        side_table, flat, from_pair
    )

    near_w, p_far = lax.optimization_barrier((near_w, p_far))
    far_in = call(rows_kernel, [smem, vmem], [row_shape], 1, "row")(turn, p_far)[0]
    far_in = lax.ppermute(far_in, "row", in_way)

    def send(place, way):
        return [lax.ppermute(later[3 * s - 3 + place], "col", way) for s in range(1, operators)]

    w_own, later = lax.optimization_barrier((w_own, later))
    far_a = [send(0, far_way)]
    near_a = send(2, near_way)

    result = None
    for s in range(operators):
        own_w, far_w, sums = [None, None], [None, None], [None, None]
        if s == 0:
            sums[0], flat, far_w[0], own_w[0] = call(
                functools.partial(first_outer_kernel, operators),
                [smem, smem, smem] + [vmem] * 9,
                [part_shape, flat_shape, w_shape, w_shape],
                LONG,
                "first_outer",
                aliases={11: 1},
            )(own_table, side_table, turn, a_vals, from_pair, w_own[0][0], near_w, p_vals, p_near, p_far, far_out, flat)
            sums[1], flat, far_w[1], own_w[1], inner_w = call(
                functools.partial(first_inner_kernel, operators),
                [smem, smem, smem] + [vmem] * 8,
                [part_shape, flat_shape, w_shape, w_shape, w_shape],
                LONG,
                "first_inner",
                aliases={10: 1},
            )(own_table, side_table, turn, a_vals, from_pair, w_own[1][0], p_vals, p_near, p_far, far_in, flat)
            near_w = [near_w, inner_w]
            inner_w, later = lax.optimization_barrier((inner_w, later))
            far_a.append(send(1, far_way))
            a_sides = [None] + [[(near_a[s], far_a[x][s]) for x in range(2)] for s in range(operators - 1)]
        else:
            near_w = [None, None]
            for x in range(2):
                if x == 1:
                    from_out, w_own = lax.optimization_barrier((from_out, w_own))
                sums[x], near_w[x], far_w[x], own_w[x] = call(
                    functools.partial(sides_kernel, operators, s, x),
                    [smem, smem, smem] + [vmem] * 8,
                    [part_shape, w_shape, w_shape, w_shape],
                    100,
                    "sides",
                )(own_table, side_table, turn, a_vals, *a_sides[s][x], flat, w_own[x][s], p_vals, p_near, p_far)
        from_out = lax.ppermute(sums[0], "row", out_way)
        from_in = lax.ppermute(sums[1], "row", in_way)
        centre = call(
            centre_kernel,
            [smem] + [vmem] * 11,
            jax.ShapeDtypeStruct((3, 5, block, block), f32),
            144,
            "centre",
        )(turn, p_vals, p_near, p_far, *far_w, *own_w, w_own[0][s], w_own[1][s], *near_w)
        result = call(
            functools.partial(final_kernel, s),
            [smem] + [vmem] * 3 + ([any_spec] if s else []),
            jax.ShapeDtypeStruct((operators, 1, 1, 25, block, block), bf16),
            1,
            "final",
            [pltpu.VMEM((5, 5, block, block), bf16), pltpu.SemaphoreType.DMA((5,))],
            aliases={4: 0} if s else None,
            out_spec=any_spec,
        )(turn, centre, from_out, from_in, *([result] if s else []))
    return result


def solution(mesh):
    placed = (
        P(None, "row", "col", None, None, None),
        P(None, "row", "col", None),
        P(None, "row", "col"),
        P("row", "col", None, None, None),
    )
    return jax.shard_map(
        per_device,
        mesh=mesh,
        in_specs=placed,
        out_specs=P(None, "row", "col", None, None, None),
        check_vma=False,
    )
```

```python
import functools

import jax
import jax.numpy as jnp
from jax import lax
from jax.experimental import pallas as pl
from jax.experimental.pallas import tpu as pltpu
from jax.sharding import PartitionSpec as P

FAR, OWN_0, OWN_1, NEAR = range(4)
HALF = 32
ZERO = 3 * HALF
INFO = 16
LONG = 10**11
VMEM_LIMIT = 24 * 1024 * 1024


def pair(count):
    return [(i, i ^ 1) for i in range(count)]


def outward(count):
    return [(i, (i + (1 if i % 2 else -1)) % count) for i in range(count)]


def aside(count):
    return [(i, (i + (2 if i % 2 else -2)) % count) for i in range(count)]


def onward(count):
    return [(i, (i + (-2 if i % 2 else 2)) % count) for i in range(count)]


def table_kernel(operators, roles, turn, *refs):
    table = refs[-1]
    odd, flip = turns(turn)
    each = 2 * operators
    wide = table.shape[1] // 9 + 1
    parts = []
    for place in range(2):
        array = refs[min(place, len(refs) - 2)]
        last = array.shape[0] - (INFO if len(refs) == 2 and place == 0 else 0)
        parts.append(array[last - INFO : last, :].astype(jnp.float32)[:each, :wide])
    info = jnp.concatenate(parts, axis=0).astype(jnp.int32)
    slots = info.shape[1] - 1
    shape = table.shape
    row = lax.broadcasted_iota(jnp.int32, shape, 0)
    place = lax.broadcasted_iota(jnp.int32, shape, 1)
    slot = place // 9
    band = place - 9 * slot
    band_y = band // 3
    band_x = band - 3 * band_y
    fine_x = row & 1
    fine_y = jnp.where(row < each, roles[0], roles[1]) - 1
    off = jnp.zeros(shape, jnp.int32)
    for k in range(slots):
        off = off + jnp.where(slot == k, info[:, k : k + 1], 0)
    off_x = jnp.where(off >= 6, 2, jnp.where(off >= 3, 1, 0))
    near_x = fine_x + (off_x - 1) * (1 - 2 * flip)
    near_y = fine_y + (off - 3 * off_x - 1) * (1 - 2 * odd)
    place_x = band_x - (((near_x - 1) >> 1) - (fine_x >> 1) + 1)
    place_y = band_y - (((near_y - 1) >> 1) - (fine_y >> 1) + 1)
    corner_x = jnp.where((near_x & 1) == 1, place_x, 1 - place_x)
    corner_y = jnp.where((near_y & 1) == 1, place_y, 1 - place_y)
    good = (place_x >= 0) & (place_x < 2) & (place_y >= 0) & (place_y < 2)
    good = good & (slot < info[:, slots:])
    side = jnp.where(near_y < 0, 2 * HALF, jnp.where(near_y < 2, 0, HALF))
    index = side + (near_x + 1) * 8 + ((near_y & 1) ^ odd) * 4 + 2 * corner_x + corner_y
    table[...] = jnp.where(good, index, ZERO)


def table_row(operators, role, operator, x):
    return (operators if role in (OWN_1, FAR) else 0) * 2 + operator * 2 + x


def turns(turn):
    return turn[0] & 1, turn[0] >> 1


def fill(flat, first, rows):
    for x, piece, at in rows:
        for y in range(2):
            flat[pl.ds(first + 8 * (x + 1) + 4 * y, 4)] = piece[at, y]


def rows_kernel(turn, piece, *outs):
    flip = turns(turn)[1]
    for out, x in zip(outs, (1 - flip, flip)):
        out[0] = piece[x]


def pack_column(turn, off, count, a_own, y, out):
    operators, _, _, slots = off.shape
    block = a_own.shape[-1]
    flip = turns(turn)[1]
    row = lax.broadcasted_iota(jnp.int32, (INFO, block), 0)
    lane = lax.broadcasted_iota(jnp.int32, (INFO, block), 1)
    for x in range(2):
        for k in range(slots):
            out[pl.ds((x * slots + k) * block, block), :] = a_own[0, x ^ flip, y, k]
    line = jnp.zeros((INFO, block), jnp.int32)
    for s in range(operators):
        for x in range(2):
            here = row == 2 * s + x
            line = jnp.where(here & (lane == slots), count[s, x ^ flip, y], line)
            for k in range(slots):
                line = jnp.where(here & (lane == k), off[s, x ^ flip, y, k], line)
    out[pl.ds(2 * slots * block, INFO), :] = line.astype(jnp.float32).astype(out.dtype)


def pack_far_kernel(turn, off, count, a_own, out):
    pack_column(turn, off, count, a_own, turns(turn)[0], out)


def pack_kernel(turn, off, count, a_own, after, own_1, *later):
    odd, flip = turns(turn)
    for s in range(1, a_own.shape[0]):
        far_0, far_1, near = later[3 * s - 3 : 3 * s]
        for x, far in enumerate((far_0, far_1)):
            far[...] = a_own[s, x ^ flip, odd]
            near[x] = a_own[s, x ^ flip, 1 - odd]
    pack_column(turn, off, count, a_own, 1 - odd, own_1)


def join_kernel(near, far, out):
    count = near.shape[0] - INFO
    out[pl.ds(0, count), :] = near[pl.ds(0, count), :]
    out[pl.ds(count, count), :] = far[pl.ds(0, count), :]
    out[pl.ds(2 * count, INFO), :] = near[pl.ds(count, INFO), :]
    out[pl.ds(2 * count + INFO, INFO), :] = far[pl.ds(count, INFO), :]


def joined_row(joined, side, x):
    block = joined.shape[1]
    slots = joined.shape[0] // (4 * block)
    first = (side * 2 + x) * slots
    return [joined.at[pl.ds((first + k) * block, block), :] for k in range(slots)]


def row_of(array):
    return [array.at[k] for k in range(array.shape[0])]


def fine_row(table, number, flat, blocks, w_ref):
    slots = len(blocks)
    left = jnp.concatenate([ref[...] for ref in blocks], axis=1)
    for band_y in range(3):
        right = jnp.concatenate(
            [
                jnp.concatenate(
                    [flat[table[number, k * 9 + band_y * 3 + band_x]] for band_x in range(3)], axis=1
                )
                for k in range(slots)
            ],
            axis=0,
        )
        w_ref[band_y] = jnp.dot(left, right, preferred_element_type=jnp.float32).astype(w_ref.dtype)


def coarse_column(turn, pieces, w_refs, fine_rows, lag_y, corner_x):
    odd, flip = turns(turn)
    lefts, rights = [], []
    for fine_x in fine_rows:
        for role in range(4):
            fine_y = role - 1
            band_y = lag_y - (fine_y // 2 + 1)
            if 0 <= band_y < 3:
                corner_y = 1 if role in (FAR, NEAR) else 0
                lefts.append(pieces[role][fine_x ^ flip, (fine_y & 1) ^ odd, corner_x + corner_y])
                rights.append(w_refs[role][fine_x][band_y])
    left = jnp.concatenate(lefts, axis=0)
    right = jnp.concatenate(rights, axis=0)
    return lax.dot_general(left, right, (((0,), (0,)), ((), ())), preferred_element_type=jnp.float32)


def edge(turn, pieces, w_refs, fine_x, out):
    block = out.shape[-1]
    for lag_y in range(5):
        total = coarse_column(turn, pieces, w_refs, (fine_x,), lag_y, 2)
        for lag_x in range(3):
            out[lag_x, lag_y] = total[:, lag_x * block : (lag_x + 1) * block].astype(out.dtype)


def near_own_kernel(operators, table, turn, a_own, p_own, p_near, own_out, own_in, near_out, near_in, flat, *w_refs):
    odd, flip = turns(turn)
    fill(flat, 0, ((-1, own_out, 0), (0, p_own, flip), (1, p_own, 1 - flip), (2, own_in, 0)))
    fill(flat, HALF, ((-1, near_out, 0), (0, p_near, flip), (1, p_near, 1 - flip), (2, near_in, 0)))
    flat[ZERO] = jnp.zeros(flat.shape[1:], flat.dtype)
    for s in range(operators):
        for x in range(2):
            fine_row(
                table, table_row(operators, OWN_1, s, x), flat, row_of(a_own.at[s, x ^ flip, 1 - odd]), w_refs[2 * s + x]
            )


def near_kernel(operators, table, flat, a_pair, w_ref):
    fine_row(table, table_row(operators, NEAR, 0, 0), flat, joined_row(a_pair, 0, 0), w_ref)


def first_outer_kernel(
    operators, own_table, table, turn, a_own, a_pair, w_own, w_near, p_own, p_near, p_far, far_out, held, out, flat, w_far, w_own_0
):
    odd, flip = turns(turn)
    fill(flat, 2 * HALF, ((-1, far_out, 0), (0, p_far, flip), (1, p_far, 1 - flip)))
    fine_row(table, table_row(operators, FAR, 0, 0), flat, joined_row(a_pair, 1, 0), w_far)
    fine_row(own_table, table_row(operators, OWN_0, 0, 0), flat, row_of(a_own.at[0, flip, odd]), w_own_0)
    edge(turn, (p_far, p_own, p_own, p_near), one_row(0, w_far, w_own_0, w_own, w_near), 0, out)


def first_inner_kernel(
    operators, own_table, table, turn, a_own, a_pair, w_own, p_own, p_near, p_far, far_in, held, out, flat, w_far, w_own_0, w_near
):
    odd, flip = turns(turn)
    fill(flat, 2 * HALF, ((2, far_in, 0),))
    fine_row(table, table_row(operators, NEAR, 0, 1), flat, joined_row(a_pair, 0, 1), w_near)
    fine_row(table, table_row(operators, FAR, 0, 1), flat, joined_row(a_pair, 1, 1), w_far)
    fine_row(own_table, table_row(operators, OWN_0, 0, 1), flat, row_of(a_own.at[0, 1 - flip, odd]), w_own_0)
    edge(turn, (p_far, p_own, p_own, p_near), one_row(1, w_far, w_own_0, w_own, w_near), 1, out)


def one_row(x, *w_refs):
    return [{x: ref} for ref in w_refs]


def sides_kernel(
    operators, operator, x, own_table, table, turn, a_own, a_near, a_far, flat, w_own, p_own, p_near, p_far, out, w_near, w_far, w_own_0
):
    odd, flip = turns(turn)
    fine_row(own_table, table_row(operators, OWN_0, operator, x), flat, row_of(a_own.at[operator, x ^ flip, odd]), w_own_0)
    fine_row(table, table_row(operators, NEAR, operator, x), flat, row_of(a_near.at[x]), w_near)
    fine_row(table, table_row(operators, FAR, operator, x), flat, row_of(a_far), w_far)
    edge(turn, (p_far, p_own, p_own, p_near), one_row(x, w_far, w_own_0, w_own, w_near), x, out)


def centre_kernel(turn, p_own, p_near, p_far, *refs):
    out = refs[-1]
    block = out.shape[-1]
    w_refs = (refs[0:2], refs[2:4], refs[4:6], refs[6:8])
    for lag_y in range(5):
        total = coarse_column(turn, (p_far, p_own, p_own, p_near), w_refs, (0, 1), lag_y, 0)
        for lag_x in range(3):
            out[lag_x, lag_y] = total[:, lag_x * block : (lag_x + 1) * block]


def final_kernel(operator, turn, own, outer, inner, *refs):
    out, total, sems = refs[-3:]
    odd, flip = turns(turn)
    copies = []
    for lag_x in range(5):
        for lag_y in range(5):
            block = None
            for part, at in ((outer, 2 - lag_x), (own, lag_x - 1), (inner, 4 - lag_x)):
                if 0 <= at < 3:
                    term = part[at, lag_y].astype(jnp.float32)
                    block = term if block is None else block + term
            total[lag_x, lag_y + odd * (4 - 2 * lag_y)] = block.astype(out.dtype)
        place = pl.ds(5 * (lag_x + flip * (4 - 2 * lag_x)), 5)
        copies.append(pltpu.make_async_copy(total.at[lag_x], out.at[operator, 0, 0, place], sems.at[lag_x]))
        copies[-1].start()
    for copy in copies:
        copy.wait()


def per_device(a_vals, a_off, a_count, p_vals):
    operators, _, _, slots, block, _ = a_vals.shape
    cols = lax.axis_size("col")
    rows = lax.axis_size("row")
    odd = (lax.axis_index("col") & 1).astype(jnp.int32)
    flip = (lax.axis_index("row") & 1).astype(jnp.int32)
    in_way, out_way = pair(rows), outward(rows)
    near_way, far_way, on_way, aside_way = pair(cols), outward(cols), onward(cols), aside(cols)

    smem = pl.BlockSpec(memory_space=pltpu.SMEM)
    any_spec = pl.BlockSpec(memory_space=pl.ANY)
    vmem = pl.BlockSpec(memory_space=pltpu.VMEM)
    bf16, f32 = jnp.bfloat16, jnp.float32
    turn = (odd + 2 * flip)[None]
    flat_shape = jax.ShapeDtypeStruct((ZERO + 1, block, block), bf16)
    w_shape = jax.ShapeDtypeStruct((3, block, 3 * block), bf16)
    part_shape = jax.ShapeDtypeStruct((3, 5, block, block), bf16)

    def call(kernel, in_specs, out_shape, products, name, scratch=(), aliases=None, limit=VMEM_LIMIT, out_spec=None):
        single = not isinstance(out_shape, list)
        return pl.pallas_call(
            kernel,
            in_specs=in_specs,
            out_specs=(out_spec or vmem) if single else [vmem] * len(out_shape),
            out_shape=out_shape,
            scratch_shapes=list(scratch),
            input_output_aliases=aliases or {},
            compiler_params=pltpu.CompilerParams(vmem_limit_bytes=limit),
            cost_estimate=pl.CostEstimate(flops=products, bytes_accessed=1024, transcendentals=0),
            name=name,
        )

    p_near = lax.ppermute(p_vals, "col", near_way)
    column = jax.ShapeDtypeStruct((2 * slots * block + INFO, block), bf16)
    slots_shape = jax.ShapeDtypeStruct((slots, block, block), bf16)
    two_slots = jax.ShapeDtypeStruct((2, slots, block, block), bf16)
    own_0 = call(pack_far_kernel, [smem] * 3 + [vmem], column, 1, "pack_far", limit=60 << 20)(
        turn, a_off, a_count, a_vals
    )
    own_1, *later = call(
        pack_kernel, [smem] * 3 + [vmem, any_spec], [column] + [slots_shape, slots_shape, two_slots] * (operators - 1), 1, "pack"
    )(turn, a_off, a_count, a_vals, own_0)
    moved = lax.ppermute(own_0, "col", aside_way)
    table_shape = jax.ShapeDtypeStruct((operators * 4, slots * 9), jnp.int32)
    own_table = call(
        functools.partial(table_kernel, operators, (OWN_0, OWN_1)), [smem, vmem, vmem], table_shape, 1, "own_table"
    )(turn, own_0, own_1)
    joined = jax.ShapeDtypeStruct((4 * slots * block + 2 * INFO, block), bf16)
    joined = call(join_kernel, [vmem, vmem], joined, 1, "join")(own_1, moved)
    row_shape = jax.ShapeDtypeStruct((1, 2, 4, block, block), bf16)
    rows_of = call(rows_kernel, [smem, vmem], [row_shape] * 2, 1, "rows")
    own_in, own_out = rows_of(turn, p_vals)
    own_in = lax.ppermute(own_in, "row", in_way)
    own_out = lax.ppermute(own_out, "row", out_way)
    p_far = lax.ppermute(p_near, "col", on_way)
    p_near, joined = lax.optimization_barrier((p_near, joined))
    from_pair = lax.ppermute(joined, "col", near_way)
    p_rows, own_in, own_out = lax.optimization_barrier((p_near, own_in, own_out))
    near_in, near_out = rows_of(turn, p_rows)
    near_in = lax.ppermute(near_in, "row", in_way)
    near_out = lax.ppermute(near_out, "row", out_way)
    far_out = lax.ppermute(near_out, "col", on_way)
    flat, *w_own = call(
        functools.partial(near_own_kernel, operators),
        [smem, smem] + [vmem] * 7,
        [flat_shape] + [w_shape] * (2 * operators),
        360,
        "near_own",
    )(own_table, turn, a_vals, p_vals, p_near, own_out, own_in, near_out, near_in)
    w_own = [w_own[0::2], w_own[1::2]]

    side_table = call(
        functools.partial(table_kernel, operators, (NEAR, FAR)), [smem, vmem], table_shape, 1, "side_table"
    )(turn, from_pair)

    near_w = call(functools.partial(near_kernel, operators), [smem, vmem, vmem], w_shape, 45, "near")(
        side_table, flat, from_pair
    )

    near_w, p_far = lax.optimization_barrier((near_w, p_far))
    far_in = call(rows_kernel, [smem, vmem], [row_shape], 1, "row")(turn, p_far)[0]
    far_in = lax.ppermute(far_in, "row", in_way)

    def send(place, way):
        return [lax.ppermute(later[3 * s - 3 + place], "col", way) for s in range(1, operators)]

    w_own, later = lax.optimization_barrier((w_own, later))
    far_a = [send(0, far_way)]
    near_a = send(2, near_way)

    result = None
    for s in range(operators):
        own_w, far_w, sums = [None, None], [None, None], [None, None]
        if s == 0:
            sums[0], flat, far_w[0], own_w[0] = call(
                functools.partial(first_outer_kernel, operators),
                [smem, smem, smem] + [vmem] * 9,
                [part_shape, flat_shape, w_shape, w_shape],
                LONG,
                "first_outer",
                aliases={11: 1},
            )(own_table, side_table, turn, a_vals, from_pair, w_own[0][0], near_w, p_vals, p_near, p_far, far_out, flat)
            sums[1], flat, far_w[1], own_w[1], inner_w = call(
                functools.partial(first_inner_kernel, operators),
                [smem, smem, smem] + [vmem] * 8,
                [part_shape, flat_shape, w_shape, w_shape, w_shape],
                LONG,
                "first_inner",
                aliases={10: 1},
            )(own_table, side_table, turn, a_vals, from_pair, w_own[1][0], p_vals, p_near, p_far, far_in, flat)
            near_w = [near_w, inner_w]
            inner_w, later = lax.optimization_barrier((inner_w, later))
            far_a.append(send(1, far_way))
            a_sides = [None] + [[(near_a[s], far_a[x][s]) for x in range(2)] for s in range(operators - 1)]
        else:
            near_w = [None, None]
            for x in range(2):
                if x == 1:
                    from_out, w_own = lax.optimization_barrier((from_out, w_own))
                sums[x], near_w[x], far_w[x], own_w[x] = call(
                    functools.partial(sides_kernel, operators, s, x),
                    [smem, smem, smem] + [vmem] * 8,
                    [part_shape, w_shape, w_shape, w_shape],
                    100,
                    "sides",
                )(own_table, side_table, turn, a_vals, *a_sides[s][x], flat, w_own[x][s], p_vals, p_near, p_far)
        from_out = lax.ppermute(sums[0], "row", out_way)
        from_in = lax.ppermute(sums[1], "row", in_way)
        centre = call(
            centre_kernel,
            [smem] + [vmem] * 11,
            jax.ShapeDtypeStruct((3, 5, block, block), f32),
            144,
            "centre",
        )(turn, p_vals, p_near, p_far, *far_w, *own_w, w_own[0][s], w_own[1][s], *near_w)
        result = call(
            functools.partial(final_kernel, s),
            [smem] + [vmem] * 3 + ([any_spec] if s else []),
            jax.ShapeDtypeStruct((operators, 1, 1, 25, block, block), bf16),
            1,
            "final",
            [pltpu.VMEM((5, 5, block, block), bf16), pltpu.SemaphoreType.DMA((5,))],
            aliases={4: 0} if s else None,
            out_spec=any_spec,
        )(turn, centre, from_out, from_in, *([result] if s else []))
    return result


def solution(mesh):
    placed = (
        P(None, "row", "col", None, None, None),
        P(None, "row", "col", None),
        P(None, "row", "col"),
        P("row", "col", None, None, None),
    )
    return jax.shard_map(
        per_device,
        mesh=mesh,
        in_specs=placed,
        out_specs=P(None, "row", "col", None, None, None),
        check_vma=False,
    )
```

```python
import functools

import jax
import jax.numpy as jnp
from jax import lax
from jax.experimental import pallas as pl
from jax.experimental.pallas import tpu as pltpu
from jax.sharding import PartitionSpec as P

FAR, OWN_0, OWN_1, NEAR = range(4)
HALF = 32
ZERO = 3 * HALF
INFO = 16
LONG = 10**11
VMEM_LIMIT = 24 * 1024 * 1024


def pair(count):
    return [(i, i ^ 1) for i in range(count)]


def outward(count):
    return [(i, (i + (1 if i % 2 else -1)) % count) for i in range(count)]


def aside(count):
    return [(i, (i + (2 if i % 2 else -2)) % count) for i in range(count)]


def onward(count):
    return [(i, (i + (-2 if i % 2 else 2)) % count) for i in range(count)]


def table_kernel(operators, roles, turn, *refs):
    table = refs[-1]
    odd, flip = turns(turn)
    each = 2 * operators
    wide = table.shape[1] // 9 + 1
    parts = []
    for place in range(2):
        array = refs[min(place, len(refs) - 2)]
        last = array.shape[0] - (INFO if len(refs) == 2 and place == 0 else 0)
        parts.append(array[last - INFO : last, :].astype(jnp.float32)[:each, :wide])
    info = jnp.concatenate(parts, axis=0).astype(jnp.int32)
    slots = info.shape[1] - 1
    shape = table.shape
    row = lax.broadcasted_iota(jnp.int32, shape, 0)
    place = lax.broadcasted_iota(jnp.int32, shape, 1)
    slot = place // 9
    band = place - 9 * slot
    band_y = band // 3
    band_x = band - 3 * band_y
    fine_x = row & 1
    fine_y = jnp.where(row < each, roles[0], roles[1]) - 1
    off = jnp.zeros(shape, jnp.int32)
    for k in range(slots):
        off = off + jnp.where(slot == k, info[:, k : k + 1], 0)
    off_x = jnp.where(off >= 6, 2, jnp.where(off >= 3, 1, 0))
    near_x = fine_x + (off_x - 1) * (1 - 2 * flip)
    near_y = fine_y + (off - 3 * off_x - 1) * (1 - 2 * odd)
    place_x = band_x - (((near_x - 1) >> 1) - (fine_x >> 1) + 1)
    place_y = band_y - (((near_y - 1) >> 1) - (fine_y >> 1) + 1)
    corner_x = jnp.where((near_x & 1) == 1, place_x, 1 - place_x)
    corner_y = jnp.where((near_y & 1) == 1, place_y, 1 - place_y)
    good = (place_x >= 0) & (place_x < 2) & (place_y >= 0) & (place_y < 2)
    good = good & (slot < info[:, slots:])
    side = jnp.where(near_y < 0, 2 * HALF, jnp.where(near_y < 2, 0, HALF))
    index = side + (near_x + 1) * 8 + ((near_y & 1) ^ odd) * 4 + 2 * corner_x + corner_y
    table[...] = jnp.where(good, index, ZERO)


def table_row(operators, role, operator, x):
    return (operators if role in (OWN_1, FAR) else 0) * 2 + operator * 2 + x


def turns(turn):
    return turn[0] & 1, turn[0] >> 1


def fill(flat, first, rows):
    for x, piece, at in rows:
        for y in range(2):
            flat[pl.ds(first + 8 * (x + 1) + 4 * y, 4)] = piece[at, y]


def rows_kernel(turn, piece, *outs):
    flip = turns(turn)[1]
    for out, x in zip(outs, (1 - flip, flip)):
        out[0] = piece[x]


def pack_column(turn, off, count, a_own, y, out):
    operators, _, _, slots = off.shape
    block = a_own.shape[-1]
    flip = turns(turn)[1]
    row = lax.broadcasted_iota(jnp.int32, (INFO, block), 0)
    lane = lax.broadcasted_iota(jnp.int32, (INFO, block), 1)
    for x in range(2):
        for k in range(slots):
            out[pl.ds((x * slots + k) * block, block), :] = a_own[0, x ^ flip, y, k]
    line = jnp.zeros((INFO, block), jnp.int32)
    for s in range(operators):
        for x in range(2):
            here = row == 2 * s + x
            line = jnp.where(here & (lane == slots), count[s, x ^ flip, y], line)
            for k in range(slots):
                line = jnp.where(here & (lane == k), off[s, x ^ flip, y, k], line)
    out[pl.ds(2 * slots * block, INFO), :] = line.astype(jnp.float32).astype(out.dtype)


def pack_far_kernel(turn, off, count, a_own, out):
    pack_column(turn, off, count, a_own, turns(turn)[0], out)


def pack_kernel(turn, off, count, a_own, after, own_1, *later):
    odd, flip = turns(turn)
    for s in range(1, a_own.shape[0]):
        far_0, far_1, near = later[3 * s - 3 : 3 * s]
        for x, far in enumerate((far_0, far_1)):
            far[...] = a_own[s, x ^ flip, odd]
            near[x] = a_own[s, x ^ flip, 1 - odd]
    pack_column(turn, off, count, a_own, 1 - odd, own_1)


def join_kernel(near, far, out):
    count = near.shape[0] - INFO
    out[pl.ds(0, count), :] = near[pl.ds(0, count), :]
    out[pl.ds(count, count), :] = far[pl.ds(0, count), :]
    out[pl.ds(2 * count, INFO), :] = near[pl.ds(count, INFO), :]
    out[pl.ds(2 * count + INFO, INFO), :] = far[pl.ds(count, INFO), :]


def joined_row(joined, side, x):
    block = joined.shape[1]
    slots = joined.shape[0] // (4 * block)
    first = (side * 2 + x) * slots
    return [joined.at[pl.ds((first + k) * block, block), :] for k in range(slots)]


def row_of(array):
    return [array.at[k] for k in range(array.shape[0])]


def fine_row(table, number, flat, blocks, w_ref):
    slots = len(blocks)
    left = jnp.concatenate([ref[...] for ref in blocks], axis=1)
    for band_y in range(3):
        right = jnp.concatenate(
            [
                jnp.concatenate(
                    [flat[table[number, k * 9 + band_y * 3 + band_x]] for band_x in range(3)], axis=1
                )
                for k in range(slots)
            ],
            axis=0,
        )
        w_ref[band_y] = jnp.dot(left, right, preferred_element_type=jnp.float32).astype(w_ref.dtype)


def coarse_column(turn, pieces, w_refs, fine_rows, lag_y, corner_x):
    odd, flip = turns(turn)
    lefts, rights = [], []
    for fine_x in fine_rows:
        for role in range(4):
            fine_y = role - 1
            band_y = lag_y - (fine_y // 2 + 1)
            if 0 <= band_y < 3:
                corner_y = 1 if role in (FAR, NEAR) else 0
                lefts.append(pieces[role][fine_x ^ flip, (fine_y & 1) ^ odd, corner_x + corner_y])
                rights.append(w_refs[role][fine_x][band_y])
    left = jnp.concatenate(lefts, axis=0)
    right = jnp.concatenate(rights, axis=0)
    return lax.dot_general(left, right, (((0,), (0,)), ((), ())), preferred_element_type=jnp.float32)


def edge(turn, pieces, w_refs, fine_x, out):
    block = out.shape[-1]
    for lag_y in range(5):
        total = coarse_column(turn, pieces, w_refs, (fine_x,), lag_y, 2)
        for lag_x in range(3):
            out[lag_x, lag_y] = total[:, lag_x * block : (lag_x + 1) * block].astype(out.dtype)


def near_own_kernel(operators, table, turn, a_own, p_own, p_near, own_out, own_in, near_out, near_in, flat, *w_refs):
    odd, flip = turns(turn)
    fill(flat, 0, ((-1, own_out, 0), (0, p_own, flip), (1, p_own, 1 - flip), (2, own_in, 0)))
    fill(flat, HALF, ((-1, near_out, 0), (0, p_near, flip), (1, p_near, 1 - flip), (2, near_in, 0)))
    flat[ZERO] = jnp.zeros(flat.shape[1:], flat.dtype)
    for s in range(operators):
        for x in range(2):
            fine_row(
                table, table_row(operators, OWN_1, s, x), flat, row_of(a_own.at[s, x ^ flip, 1 - odd]), w_refs[2 * s + x]
            )


def near_kernel(operators, table, flat, a_pair, w_ref):
    fine_row(table, table_row(operators, NEAR, 0, 0), flat, joined_row(a_pair, 0, 0), w_ref)


def first_outer_kernel(
    operators, own_table, table, turn, a_own, a_pair, w_own, w_near, p_own, p_near, p_far, far_out, held, out, flat, w_far, w_own_0
):
    odd, flip = turns(turn)
    fill(flat, 2 * HALF, ((-1, far_out, 0), (0, p_far, flip), (1, p_far, 1 - flip)))
    fine_row(table, table_row(operators, FAR, 0, 0), flat, joined_row(a_pair, 1, 0), w_far)
    fine_row(own_table, table_row(operators, OWN_0, 0, 0), flat, row_of(a_own.at[0, flip, odd]), w_own_0)
    edge(turn, (p_far, p_own, p_own, p_near), one_row(0, w_far, w_own_0, w_own, w_near), 0, out)


def first_inner_kernel(
    operators, own_table, table, turn, a_own, a_pair, w_own, p_own, p_near, p_far, far_in, held, out, flat, w_far, w_own_0, w_near
):
    odd, flip = turns(turn)
    fill(flat, 2 * HALF, ((2, far_in, 0),))
    fine_row(table, table_row(operators, NEAR, 0, 1), flat, joined_row(a_pair, 0, 1), w_near)
    fine_row(table, table_row(operators, FAR, 0, 1), flat, joined_row(a_pair, 1, 1), w_far)
    fine_row(own_table, table_row(operators, OWN_0, 0, 1), flat, row_of(a_own.at[0, 1 - flip, odd]), w_own_0)
    edge(turn, (p_far, p_own, p_own, p_near), one_row(1, w_far, w_own_0, w_own, w_near), 1, out)


def one_row(x, *w_refs):
    return [{x: ref} for ref in w_refs]


def sides_kernel(
    operators, operator, x, own_table, table, turn, a_own, a_near, a_far, flat, w_own, p_own, p_near, p_far, out, w_near, w_far, w_own_0
):
    odd, flip = turns(turn)
    fine_row(own_table, table_row(operators, OWN_0, operator, x), flat, row_of(a_own.at[operator, x ^ flip, odd]), w_own_0)
    fine_row(table, table_row(operators, NEAR, operator, x), flat, row_of(a_near.at[x]), w_near)
    fine_row(table, table_row(operators, FAR, operator, x), flat, row_of(a_far), w_far)
    edge(turn, (p_far, p_own, p_own, p_near), one_row(x, w_far, w_own_0, w_own, w_near), x, out)


def centre_kernel(turn, p_own, p_near, p_far, *refs):
    out = refs[-1]
    block = out.shape[-1]
    w_refs = (refs[0:2], refs[2:4], refs[4:6], refs[6:8])
    for lag_y in range(5):
        total = coarse_column(turn, (p_far, p_own, p_own, p_near), w_refs, (0, 1), lag_y, 0)
        for lag_x in range(3):
            out[lag_x, lag_y] = total[:, lag_x * block : (lag_x + 1) * block]


def final_kernel(operator, turn, own, outer, inner, *refs):
    out, total, sems = refs[-3:]
    odd, flip = turns(turn)
    copies = []
    for lag_x in range(5):
        for lag_y in range(5):
            block = None
            for part, at in ((outer, 2 - lag_x), (own, lag_x - 1), (inner, 4 - lag_x)):
                if 0 <= at < 3:
                    term = part[at, lag_y].astype(jnp.float32)
                    block = term if block is None else block + term
            total[lag_x, lag_y + odd * (4 - 2 * lag_y)] = block.astype(out.dtype)
        place = pl.ds(5 * (lag_x + flip * (4 - 2 * lag_x)), 5)
        copies.append(pltpu.make_async_copy(total.at[lag_x], out.at[operator, 0, 0, place], sems.at[lag_x]))
        copies[-1].start()
    for copy in copies:
        copy.wait()


def per_device(a_vals, a_off, a_count, p_vals):
    operators, _, _, slots, block, _ = a_vals.shape
    cols = lax.axis_size("col")
    rows = lax.axis_size("row")
    odd = (lax.axis_index("col") & 1).astype(jnp.int32)
    flip = (lax.axis_index("row") & 1).astype(jnp.int32)
    in_way, out_way = pair(rows), outward(rows)
    near_way, far_way, on_way, aside_way = pair(cols), outward(cols), onward(cols), aside(cols)

    smem = pl.BlockSpec(memory_space=pltpu.SMEM)
    any_spec = pl.BlockSpec(memory_space=pl.ANY)
    vmem = pl.BlockSpec(memory_space=pltpu.VMEM)
    bf16, f32 = jnp.bfloat16, jnp.float32
    turn = (odd + 2 * flip)[None]
    flat_shape = jax.ShapeDtypeStruct((ZERO + 1, block, block), bf16)
    w_shape = jax.ShapeDtypeStruct((3, block, 3 * block), bf16)
    part_shape = jax.ShapeDtypeStruct((3, 5, block, block), bf16)

    def call(kernel, in_specs, out_shape, products, name, scratch=(), aliases=None, limit=VMEM_LIMIT, out_spec=None):
        single = not isinstance(out_shape, list)
        return pl.pallas_call(
            kernel,
            in_specs=in_specs,
            out_specs=(out_spec or vmem) if single else [vmem] * len(out_shape),
            out_shape=out_shape,
            scratch_shapes=list(scratch),
            input_output_aliases=aliases or {},
            compiler_params=pltpu.CompilerParams(vmem_limit_bytes=limit),
            cost_estimate=pl.CostEstimate(flops=products, bytes_accessed=1024, transcendentals=0),
            name=name,
        )

    p_near = lax.ppermute(p_vals, "col", near_way)
    column = jax.ShapeDtypeStruct((2 * slots * block + INFO, block), bf16)
    slots_shape = jax.ShapeDtypeStruct((slots, block, block), bf16)
    two_slots = jax.ShapeDtypeStruct((2, slots, block, block), bf16)
    own_0 = call(pack_far_kernel, [smem] * 3 + [vmem], column, 1, "pack_far", limit=60 << 20)(
        turn, a_off, a_count, a_vals
    )
    own_1, *later = call(
        pack_kernel, [smem] * 3 + [vmem, any_spec], [column] + [slots_shape, slots_shape, two_slots] * (operators - 1), 1, "pack"
    )(turn, a_off, a_count, a_vals, own_0)
    moved = lax.ppermute(own_0, "col", aside_way)
    table_shape = jax.ShapeDtypeStruct((operators * 4, slots * 9), jnp.int32)
    own_table = call(
        functools.partial(table_kernel, operators, (OWN_0, OWN_1)), [smem, vmem, vmem], table_shape, 1, "own_table"
    )(turn, own_0, own_1)
    joined = jax.ShapeDtypeStruct((4 * slots * block + 2 * INFO, block), bf16)
    joined = call(join_kernel, [vmem, vmem], joined, 1, "join")(own_1, moved)
    row_shape = jax.ShapeDtypeStruct((1, 2, 4, block, block), bf16)
    rows_of = call(rows_kernel, [smem, vmem], [row_shape] * 2, 1, "rows")
    own_in, own_out = rows_of(turn, p_vals)
    own_in = lax.ppermute(own_in, "row", in_way)
    own_out = lax.ppermute(own_out, "row", out_way)
    p_far = lax.ppermute(p_near, "col", on_way)
    p_near, joined = lax.optimization_barrier((p_near, joined))
    from_pair = lax.ppermute(joined, "col", near_way)
    p_rows, own_in, own_out = lax.optimization_barrier((p_near, own_in, own_out))
    near_in, near_out = rows_of(turn, p_rows)
    near_in = lax.ppermute(near_in, "row", in_way)
    near_out = lax.ppermute(near_out, "row", out_way)
    far_out = lax.ppermute(near_out, "col", on_way)
    flat, *w_own = call(
        functools.partial(near_own_kernel, operators),
        [smem, smem] + [vmem] * 7,
        [flat_shape] + [w_shape] * (2 * operators),
        360,
        "near_own",
    )(own_table, turn, a_vals, p_vals, p_near, own_out, own_in, near_out, near_in)
    w_own = [w_own[0::2], w_own[1::2]]

    side_table = call(
        functools.partial(table_kernel, operators, (NEAR, FAR)), [smem, vmem], table_shape, 1, "side_table"
    )(turn, from_pair)

    near_w = call(functools.partial(near_kernel, operators), [smem, vmem, vmem], w_shape, 45, "near")(
        side_table, flat, from_pair
    )

    near_w, p_far = lax.optimization_barrier((near_w, p_far))
    far_in = call(rows_kernel, [smem, vmem], [row_shape], 1, "row")(turn, p_far)[0]
    far_in = lax.ppermute(far_in, "row", in_way)

    def send(place, way):
        return [lax.ppermute(later[3 * s - 3 + place], "col", way) for s in range(1, operators)]

    w_own, later = lax.optimization_barrier((w_own, later))
    far_a = [send(0, far_way)]
    near_a = send(2, near_way)

    result = None
    for s in range(operators):
        own_w, far_w, sums = [None, None], [None, None], [None, None]
        if s == 0:
            sums[0], flat, far_w[0], own_w[0] = call(
                functools.partial(first_outer_kernel, operators),
                [smem, smem, smem] + [vmem] * 9,
                [part_shape, flat_shape, w_shape, w_shape],
                LONG,
                "first_outer",
                aliases={11: 1},
            )(own_table, side_table, turn, a_vals, from_pair, w_own[0][0], near_w, p_vals, p_near, p_far, far_out, flat)
            sums[1], flat, far_w[1], own_w[1], inner_w = call(
                functools.partial(first_inner_kernel, operators),
                [smem, smem, smem] + [vmem] * 8,
                [part_shape, flat_shape, w_shape, w_shape, w_shape],
                LONG,
                "first_inner",
                aliases={10: 1},
            )(own_table, side_table, turn, a_vals, from_pair, w_own[1][0], p_vals, p_near, p_far, far_in, flat)
            near_w = [near_w, inner_w]
        else:
            near_w = [None, None]
            for x in range(2):
                if x == 1:
                    from_out, w_own = lax.optimization_barrier((from_out, w_own))
                    sums[0], later = lax.optimization_barrier((sums[0], later))
                    far_a.append(send(1, far_way))
                sums[x], near_w[x], far_w[x], own_w[x] = call(
                    functools.partial(sides_kernel, operators, s, x),
                    [smem, smem, smem] + [vmem] * 8,
                    [part_shape, w_shape, w_shape, w_shape],
                    100,
                    "sides",
                )(own_table, side_table, turn, a_vals, near_a[s - 1], far_a[x][s - 1], flat, w_own[x][s], p_vals, p_near, p_far)
        from_out = lax.ppermute(sums[0], "row", out_way)
        from_in = lax.ppermute(sums[1], "row", in_way)
        centre = call(
            centre_kernel,
            [smem] + [vmem] * 11,
            jax.ShapeDtypeStruct((3, 5, block, block), f32),
            144,
            "centre",
        )(turn, p_vals, p_near, p_far, *far_w, *own_w, w_own[0][s], w_own[1][s], *near_w)
        result = call(
            functools.partial(final_kernel, s),
            [smem] + [vmem] * 3 + ([any_spec] if s else []),
            jax.ShapeDtypeStruct((operators, 1, 1, 25, block, block), bf16),
            1,
            "final",
            [pltpu.VMEM((5, 5, block, block), bf16), pltpu.SemaphoreType.DMA((5,))],
            aliases={4: 0} if s else None,
            out_spec=any_spec,
        )(turn, centre, from_out, from_in, *([result] if s else []))
    return result


def solution(mesh):
    placed = (
        P(None, "row", "col", None, None, None),
        P(None, "row", "col", None),
        P(None, "row", "col"),
        P("row", "col", None, None, None),
    )
    return jax.shard_map(
        per_device,
        mesh=mesh,
        in_specs=placed,
        out_specs=P(None, "row", "col", None, None, None),
        check_vma=False,
    )
```

```python
import functools

import jax
import jax.numpy as jnp
from jax import lax
from jax.experimental import pallas as pl
from jax.experimental.pallas import tpu as pltpu
from jax.sharding import PartitionSpec as P

FAR, OWN_0, OWN_1, NEAR = range(4)
HALF = 32
ZERO = 3 * HALF
INFO = 16
LONG = 10**11
VMEM_LIMIT = 16 * 1024 * 1024


def pair(count):
    return [(i, i ^ 1) for i in range(count)]


def outward(count):
    return [(i, (i + (1 if i % 2 else -1)) % count) for i in range(count)]


def aside(count):
    return [(i, (i + (2 if i % 2 else -2)) % count) for i in range(count)]


def onward(count):
    return [(i, (i + (-2 if i % 2 else 2)) % count) for i in range(count)]


def table_kernel(operators, roles, turn, *refs):
    table = refs[-1]
    odd, flip = turns(turn)
    each = 2 * operators
    wide = table.shape[1] // 9 + 1
    parts = []
    for place in range(2):
        array = refs[min(place, len(refs) - 2)]
        last = array.shape[0] - (INFO if len(refs) == 2 and place == 0 else 0)
        parts.append(array[last - INFO : last, :].astype(jnp.float32)[:each, :wide])
    info = jnp.concatenate(parts, axis=0).astype(jnp.int32)
    slots = info.shape[1] - 1
    shape = table.shape
    row = lax.broadcasted_iota(jnp.int32, shape, 0)
    place = lax.broadcasted_iota(jnp.int32, shape, 1)
    slot = place // 9
    band = place - 9 * slot
    band_y = band // 3
    band_x = band - 3 * band_y
    fine_x = row & 1
    fine_y = jnp.where(row < each, roles[0], roles[1]) - 1
    off = jnp.zeros(shape, jnp.int32)
    for k in range(slots):
        off = off + jnp.where(slot == k, info[:, k : k + 1], 0)
    off_x = jnp.where(off >= 6, 2, jnp.where(off >= 3, 1, 0))
    near_x = fine_x + (off_x - 1) * (1 - 2 * flip)
    near_y = fine_y + (off - 3 * off_x - 1) * (1 - 2 * odd)
    place_x = band_x - (((near_x - 1) >> 1) - (fine_x >> 1) + 1)
    place_y = band_y - (((near_y - 1) >> 1) - (fine_y >> 1) + 1)
    corner_x = jnp.where((near_x & 1) == 1, place_x, 1 - place_x)
    corner_y = jnp.where((near_y & 1) == 1, place_y, 1 - place_y)
    good = (place_x >= 0) & (place_x < 2) & (place_y >= 0) & (place_y < 2)
    good = good & (slot < info[:, slots:])
    side = jnp.where(near_y < 0, 2 * HALF, jnp.where(near_y < 2, 0, HALF))
    index = side + (near_x + 1) * 8 + ((near_y & 1) ^ odd) * 4 + 2 * corner_x + corner_y
    table[...] = jnp.where(good, index, ZERO)


def table_row(operators, role, operator, x):
    return (operators if role in (OWN_1, FAR) else 0) * 2 + operator * 2 + x


def turns(turn):
    return turn[0] & 1, turn[0] >> 1


def fill(flat, first, rows):
    for x, piece, at in rows:
        for y in range(2):
            flat[pl.ds(first + 8 * (x + 1) + 4 * y, 4)] = piece[at, y]


def rows_kernel(turn, piece, *outs):
    flip = turns(turn)[1]
    for out, x in zip(outs, (1 - flip, flip)):
        out[0] = piece[x]


def pack_column(turn, off, count, a_own, y, out):
    operators, _, _, slots = off.shape
    block = a_own.shape[-1]
    flip = turns(turn)[1]
    row = lax.broadcasted_iota(jnp.int32, (INFO, block), 0)
    lane = lax.broadcasted_iota(jnp.int32, (INFO, block), 1)
    for x in range(2):
        for k in range(slots):
            out[pl.ds((x * slots + k) * block, block), :] = a_own[0, x ^ flip, y, k]
    line = jnp.zeros((INFO, block), jnp.int32)
    for s in range(operators):
        for x in range(2):
            here = row == 2 * s + x
            line = jnp.where(here & (lane == slots), count[s, x ^ flip, y], line)
            for k in range(slots):
                line = jnp.where(here & (lane == k), off[s, x ^ flip, y, k], line)
    out[pl.ds(2 * slots * block, INFO), :] = line.astype(jnp.float32).astype(out.dtype)


def pack_far_kernel(turn, off, count, a_own, out):
    pack_column(turn, off, count, a_own, turns(turn)[0], out)


def pack_kernel(turn, off, count, a_own, after, own_1, *later):
    odd, flip = turns(turn)
    for s in range(1, a_own.shape[0]):
        far_0, far_1, near = later[3 * s - 3 : 3 * s]
        for x, far in enumerate((far_0, far_1)):
            far[...] = a_own[s, x ^ flip, odd]
            near[x] = a_own[s, x ^ flip, 1 - odd]
    pack_column(turn, off, count, a_own, 1 - odd, own_1)


def join_kernel(near, far, out):
    count = near.shape[0] - INFO
    out[pl.ds(0, count), :] = near[pl.ds(0, count), :]
    out[pl.ds(count, count), :] = far[pl.ds(0, count), :]
    out[pl.ds(2 * count, INFO), :] = near[pl.ds(count, INFO), :]
    out[pl.ds(2 * count + INFO, INFO), :] = far[pl.ds(count, INFO), :]


def joined_row(joined, side, x):
    block = joined.shape[1]
    slots = joined.shape[0] // (4 * block)
    first = (side * 2 + x) * slots
    return [joined.at[pl.ds((first + k) * block, block), :] for k in range(slots)]


def row_of(array):
    return [array.at[k] for k in range(array.shape[0])]


def fine_row(table, number, flat, blocks, w_ref):
    slots = len(blocks)
    left = jnp.concatenate([ref[...] for ref in blocks], axis=1)
    for band_y in range(3):
        right = jnp.concatenate(
            [
                jnp.concatenate(
                    [flat[table[number, k * 9 + band_y * 3 + band_x]] for band_x in range(3)], axis=1
                )
                for k in range(slots)
            ],
            axis=0,
        )
        w_ref[band_y] = jnp.dot(left, right, preferred_element_type=jnp.float32).astype(w_ref.dtype)


def coarse_column(turn, pieces, w_refs, fine_rows, lag_y, corner_x):
    odd, flip = turns(turn)
    lefts, rights = [], []
    for fine_x in fine_rows:
        for role in range(4):
            fine_y = role - 1
            band_y = lag_y - (fine_y // 2 + 1)
            if 0 <= band_y < 3:
                corner_y = 1 if role in (FAR, NEAR) else 0
                lefts.append(pieces[role][fine_x ^ flip, (fine_y & 1) ^ odd, corner_x + corner_y])
                rights.append(w_refs[role][fine_x][band_y])
    left = jnp.concatenate(lefts, axis=0)
    right = jnp.concatenate(rights, axis=0)
    return lax.dot_general(left, right, (((0,), (0,)), ((), ())), preferred_element_type=jnp.float32)


def edge(turn, pieces, w_refs, fine_x, out):
    block = out.shape[-1]
    for lag_y in range(5):
        total = coarse_column(turn, pieces, w_refs, (fine_x,), lag_y, 2)
        for lag_x in range(3):
            out[lag_x, lag_y] = total[:, lag_x * block : (lag_x + 1) * block].astype(out.dtype)


def near_own_kernel(operators, table, turn, a_own, p_own, p_near, own_out, own_in, near_out, near_in, flat, *w_refs):
    odd, flip = turns(turn)
    fill(flat, 0, ((-1, own_out, 0), (0, p_own, flip), (1, p_own, 1 - flip), (2, own_in, 0)))
    fill(flat, HALF, ((-1, near_out, 0), (0, p_near, flip), (1, p_near, 1 - flip), (2, near_in, 0)))
    flat[ZERO] = jnp.zeros(flat.shape[1:], flat.dtype)
    for s in range(operators):
        for x in range(2):
            fine_row(
                table, table_row(operators, OWN_1, s, x), flat, row_of(a_own.at[s, x ^ flip, 1 - odd]), w_refs[2 * s + x]
            )


def near_kernel(operators, table, flat, a_pair, w_ref):
    fine_row(table, table_row(operators, NEAR, 0, 0), flat, joined_row(a_pair, 0, 0), w_ref)


def first_outer_kernel(
    operators, own_table, table, turn, a_own, a_pair, w_own, w_near, p_own, p_near, p_far, far_out, held, out, flat, w_far, w_own_0
):
    odd, flip = turns(turn)
    fill(flat, 2 * HALF, ((-1, far_out, 0), (0, p_far, flip), (1, p_far, 1 - flip)))
    fine_row(table, table_row(operators, FAR, 0, 0), flat, joined_row(a_pair, 1, 0), w_far)
    fine_row(own_table, table_row(operators, OWN_0, 0, 0), flat, row_of(a_own.at[0, flip, odd]), w_own_0)
    edge(turn, (p_far, p_own, p_own, p_near), one_row(0, w_far, w_own_0, w_own, w_near), 0, out)


def first_inner_kernel(
    operators, own_table, table, turn, a_own, a_pair, w_own, p_own, p_near, p_far, far_in, held, out, flat, w_far, w_own_0, w_near
):
    odd, flip = turns(turn)
    fill(flat, 2 * HALF, ((2, far_in, 0),))
    fine_row(table, table_row(operators, NEAR, 0, 1), flat, joined_row(a_pair, 0, 1), w_near)
    fine_row(table, table_row(operators, FAR, 0, 1), flat, joined_row(a_pair, 1, 1), w_far)
    fine_row(own_table, table_row(operators, OWN_0, 0, 1), flat, row_of(a_own.at[0, 1 - flip, odd]), w_own_0)
    edge(turn, (p_far, p_own, p_own, p_near), one_row(1, w_far, w_own_0, w_own, w_near), 1, out)


def one_row(x, *w_refs):
    return [{x: ref} for ref in w_refs]


def sides_kernel(
    operators, operator, x, own_table, table, turn, a_own, a_near, a_far, flat, w_own, p_own, p_near, p_far, out, w_near, w_far, w_own_0
):
    odd, flip = turns(turn)
    fine_row(own_table, table_row(operators, OWN_0, operator, x), flat, row_of(a_own.at[operator, x ^ flip, odd]), w_own_0)
    fine_row(table, table_row(operators, NEAR, operator, x), flat, row_of(a_near.at[x]), w_near)
    fine_row(table, table_row(operators, FAR, operator, x), flat, row_of(a_far), w_far)
    edge(turn, (p_far, p_own, p_own, p_near), one_row(x, w_far, w_own_0, w_own, w_near), x, out)


def centre_kernel(turn, p_own, p_near, p_far, *refs):
    out = refs[-1]
    block = out.shape[-1]
    w_refs = (refs[0:2], refs[2:4], refs[4:6], refs[6:8])
    for lag_y in range(5):
        total = coarse_column(turn, (p_far, p_own, p_own, p_near), w_refs, (0, 1), lag_y, 0)
        for lag_x in range(3):
            out[lag_x, lag_y] = total[:, lag_x * block : (lag_x + 1) * block]


def final_kernel(operator, turn, own, outer, inner, *refs):
    out, total, sems = refs[-3:]
    odd, flip = turns(turn)
    copies = []
    for lag_x in range(5):
        for lag_y in range(5):
            block = None
            for part, at in ((outer, 2 - lag_x), (own, lag_x - 1), (inner, 4 - lag_x)):
                if 0 <= at < 3:
                    term = part[at, lag_y].astype(jnp.float32)
                    block = term if block is None else block + term
            total[lag_x, lag_y + odd * (4 - 2 * lag_y)] = block.astype(out.dtype)
        place = pl.ds(5 * (lag_x + flip * (4 - 2 * lag_x)), 5)
        copies.append(pltpu.make_async_copy(total.at[lag_x], out.at[operator, 0, 0, place], sems.at[lag_x]))
        copies[-1].start()
    for copy in copies:
        copy.wait()


def per_device(a_vals, a_off, a_count, p_vals):
    operators, _, _, slots, block, _ = a_vals.shape
    cols = lax.axis_size("col")
    rows = lax.axis_size("row")
    odd = (lax.axis_index("col") & 1).astype(jnp.int32)
    flip = (lax.axis_index("row") & 1).astype(jnp.int32)
    in_way, out_way = pair(rows), outward(rows)
    near_way, far_way, on_way, aside_way = pair(cols), outward(cols), onward(cols), aside(cols)

    smem = pl.BlockSpec(memory_space=pltpu.SMEM)
    any_spec = pl.BlockSpec(memory_space=pl.ANY)
    vmem = pl.BlockSpec(memory_space=pltpu.VMEM)
    bf16, f32 = jnp.bfloat16, jnp.float32
    turn = (odd + 2 * flip)[None]
    flat_shape = jax.ShapeDtypeStruct((ZERO + 1, block, block), bf16)
    w_shape = jax.ShapeDtypeStruct((3, block, 3 * block), bf16)
    part_shape = jax.ShapeDtypeStruct((3, 5, block, block), bf16)

    def call(kernel, in_specs, out_shape, products, name, scratch=(), aliases=None, limit=VMEM_LIMIT, out_spec=None):
        single = not isinstance(out_shape, list)
        return pl.pallas_call(
            kernel,
            in_specs=in_specs,
            out_specs=(out_spec or vmem) if single else [vmem] * len(out_shape),
            out_shape=out_shape,
            scratch_shapes=list(scratch),
            input_output_aliases=aliases or {},
            compiler_params=pltpu.CompilerParams(vmem_limit_bytes=limit),
            cost_estimate=pl.CostEstimate(flops=products, bytes_accessed=1024, transcendentals=0),
            name=name,
        )

    p_near = lax.ppermute(p_vals, "col", near_way)
    column = jax.ShapeDtypeStruct((2 * slots * block + INFO, block), bf16)
    slots_shape = jax.ShapeDtypeStruct((slots, block, block), bf16)
    two_slots = jax.ShapeDtypeStruct((2, slots, block, block), bf16)
    own_0 = call(pack_far_kernel, [smem] * 3 + [vmem], column, 1, "pack_far", limit=60 << 20)(
        turn, a_off, a_count, a_vals
    )
    own_1, *later = call(
        pack_kernel, [smem] * 3 + [vmem, any_spec], [column] + [slots_shape, slots_shape, two_slots] * (operators - 1), 1, "pack"
    )(turn, a_off, a_count, a_vals, own_0)
    moved = lax.ppermute(own_0, "col", aside_way)
    table_shape = jax.ShapeDtypeStruct((operators * 4, slots * 9), jnp.int32)
    own_table = call(
        functools.partial(table_kernel, operators, (OWN_0, OWN_1)), [smem, vmem, vmem], table_shape, 1, "own_table"
    )(turn, own_0, own_1)
    joined = jax.ShapeDtypeStruct((4 * slots * block + 2 * INFO, block), bf16)
    joined = call(join_kernel, [vmem, vmem], joined, 1, "join")(own_1, moved)
    row_shape = jax.ShapeDtypeStruct((1, 2, 4, block, block), bf16)
    rows_of = call(rows_kernel, [smem, vmem], [row_shape] * 2, 1, "rows")
    own_in, own_out = rows_of(turn, p_vals)
    own_in = lax.ppermute(own_in, "row", in_way)
    own_out = lax.ppermute(own_out, "row", out_way)
    p_far = lax.ppermute(p_near, "col", on_way)
    p_near, joined = lax.optimization_barrier((p_near, joined))
    from_pair = lax.ppermute(joined, "col", near_way)
    p_rows, own_in, own_out = lax.optimization_barrier((p_near, own_in, own_out))
    near_in, near_out = rows_of(turn, p_rows)
    near_in = lax.ppermute(near_in, "row", in_way)
    near_out = lax.ppermute(near_out, "row", out_way)
    far_out = lax.ppermute(near_out, "col", on_way)
    flat, *w_own = call(
        functools.partial(near_own_kernel, operators),
        [smem, smem] + [vmem] * 7,
        [flat_shape] + [w_shape] * (2 * operators),
        360,
        "near_own",
    )(own_table, turn, a_vals, p_vals, p_near, own_out, own_in, near_out, near_in)
    w_own = [w_own[0::2], w_own[1::2]]

    side_table = call(
        functools.partial(table_kernel, operators, (NEAR, FAR)), [smem, vmem], table_shape, 1, "side_table"
    )(turn, from_pair)

    near_w = call(functools.partial(near_kernel, operators), [smem, vmem, vmem], w_shape, 45, "near")(
        side_table, flat, from_pair
    )

    near_w, p_far = lax.optimization_barrier((near_w, p_far))
    far_in = call(rows_kernel, [smem, vmem], [row_shape], 1, "row")(turn, p_far)[0]
    far_in = lax.ppermute(far_in, "row", in_way)

    def send(place, way):
        return [lax.ppermute(later[3 * s - 3 + place], "col", way) for s in range(1, operators)]

    w_own, later = lax.optimization_barrier((w_own, later))
    far_a = [send(0, far_way)]
    near_a = send(2, near_way)

    result = None
    for s in range(operators):
        own_w, far_w, sums = [None, None], [None, None], [None, None]
        if s == 0:
            sums[0], flat, far_w[0], own_w[0] = call(
                functools.partial(first_outer_kernel, operators),
                [smem, smem, smem] + [vmem] * 9,
                [part_shape, flat_shape, w_shape, w_shape],
                LONG,
                "first_outer",
                aliases={11: 1},
            )(own_table, side_table, turn, a_vals, from_pair, w_own[0][0], near_w, p_vals, p_near, p_far, far_out, flat)
            sums[1], flat, far_w[1], own_w[1], inner_w = call(
                functools.partial(first_inner_kernel, operators),
                [smem, smem, smem] + [vmem] * 8,
                [part_shape, flat_shape, w_shape, w_shape, w_shape],
                LONG,
                "first_inner",
                aliases={10: 1},
            )(own_table, side_table, turn, a_vals, from_pair, w_own[1][0], p_vals, p_near, p_far, far_in, flat)
            near_w = [near_w, inner_w]
            inner_w, later = lax.optimization_barrier((inner_w, later))
            far_a.append(send(1, far_way))
            a_sides = [None] + [[(near_a[s], far_a[x][s]) for x in range(2)] for s in range(operators - 1)]
        else:
            near_w = [None, None]
            for x in range(2):
                if x == 1:
                    from_out, w_own = lax.optimization_barrier((from_out, w_own))
                sums[x], near_w[x], far_w[x], own_w[x] = call(
                    functools.partial(sides_kernel, operators, s, x),
                    [smem, smem, smem] + [vmem] * 8,
                    [part_shape, w_shape, w_shape, w_shape],
                    100,
                    "sides",
                )(own_table, side_table, turn, a_vals, *a_sides[s][x], flat, w_own[x][s], p_vals, p_near, p_far)
        from_out = lax.ppermute(sums[0], "row", out_way)
        from_in = lax.ppermute(sums[1], "row", in_way)
        centre = call(
            centre_kernel,
            [smem] + [vmem] * 11,
            jax.ShapeDtypeStruct((3, 5, block, block), f32),
            144,
            "centre",
        )(turn, p_vals, p_near, p_far, *far_w, *own_w, w_own[0][s], w_own[1][s], *near_w)
        result = call(
            functools.partial(final_kernel, s),
            [smem] + [vmem] * 3 + ([any_spec] if s else []),
            jax.ShapeDtypeStruct((operators, 1, 1, 25, block, block), bf16),
            1,
            "final",
            [pltpu.VMEM((5, 5, block, block), bf16), pltpu.SemaphoreType.DMA((5,))],
            aliases={4: 0} if s else None,
            out_spec=any_spec,
        )(turn, centre, from_out, from_in, *([result] if s else []))
    return result


def solution(mesh):
    placed = (
        P(None, "row", "col", None, None, None),
        P(None, "row", "col", None),
        P(None, "row", "col"),
        P("row", "col", None, None, None),
    )
    return jax.shard_map(
        per_device,
        mesh=mesh,
        in_specs=placed,
        out_specs=P(None, "row", "col", None, None, None),
        check_vma=False,
    )
```
